128 devices in a mesh: dp: 8 (over z, core), seq: 16 (over x, y).
Axes of the slice: x: 4, y: 4, z: 4, core: 2. Of those that a mesh axis runs over, the one named last changes fastest.
Arguments:
- queries: bfloat16 [8, 4096, 2048], P('dp', 'seq'), may hold values from -6 to 6, as said below
- keys: bfloat16 [8, 4096, 2048], P('dp', 'seq'), may hold values from -6 to 6
- values: bfloat16 [8, 4096, 2048], P('dp', 'seq'), may hold values from -6 to 6
- weight_out: bfloat16 [2048, 2048], P('dp'), may hold values from -0.125 to 0.125
- cotangent: bfloat16 [8, 4096, 2048], P('dp', 'seq'), may hold values from -6 to 6
- hidden_mask: int32 [8, 4096], P('dp', 'seq'), may hold values 0 or 1
- pattern: int32 [16, 32, 16], replicated, may hold values from 0 to 31, as said below
- live_slots: int32 [16, 32], replicated, may hold values from 1 to 16, as said below
Outputs:
- block_out: bfloat16 [8, 4096, 2048], P('dp', 'seq')
- grad_queries: bfloat16 [8, 4096, 2048], P('dp', 'seq')
- grad_keys: bfloat16 [8, 4096, 2048], P('dp', 'seq')
- grad_values: bfloat16 [8, 4096, 2048], P('dp', 'seq')
- weight_grad: float32 [2048, 2048], P('seq', 'dp')
The draws below stay inside these ranges and needn't reach their ends.
Inputs may be any that keep to these rules, and one draw needn't show every extreme that they name: `queries`: queries and keys lie within the range. pattern[h, b] holds 16 distinct block numbers; slot 0 is b itself. Slots 0 to live_slots[h, b] - 1 of pattern[h, b] are used; every head has a query block with all 16 used.
All inputs are finite; a program needn't handle non-finite values. No bound on the sum of `hidden_mask` on one device may be relied on, other than what follows from the above.
Results may differ from the reference program's by a relative error of at most 0.0098.
Values may be sent and summed in bfloat16 or wider, within the bound.
A program may use at most 128 MiB of HBM per device.

```python
import math
import jax
import jax.numpy as jnp
from jax import lax

H = 16
HD = 128
BLOCK = 128
KMAX = 16
D = 2048
LEN = 4096
NB = 32
RECS = 8


def paired_fields(key):
    base = jax.random.fold_in(key, 11)
    key_q, key_k = jax.random.split(base, 2)
    field_q = jnp.clip(jax.random.normal(key_q, (RECS, LEN, D), jnp.float32), -6.0, 6.0)
    field_k = jnp.clip(jax.random.normal(key_k, (RECS, LEN, D), jnp.float32), -6.0, 6.0)
    return (field_q, field_k)


def draw_queries(key, part):
    field_q, field_k = paired_fields(key)
    return field_q.astype(jnp.bfloat16)


def draw_keys(key, part):
    field_q, field_k = paired_fields(key)
    return field_k.astype(jnp.bfloat16)


def draw_pattern(key, part):
    raw = jax.random.randint(jax.random.fold_in(key, 3), (H, NB, NB), 0, 1 << 20)
    column = jnp.arange(NB, dtype=jnp.int32)
    ranked = raw * NB + column[None, None, :]
    own = column[:, None] == column[None, :]
    ranked = jnp.where(own[None, :, :], jnp.int32(1 << 30), ranked)
    top_vals, chosen = lax.top_k(ranked, KMAX)
    return chosen.astype(jnp.int32)


def draw_live_slots(key, part):
    key_level, key_raw, key_full = jax.random.split(jax.random.fold_in(key, 5), 3)
    level = jax.random.randint(key_level, (H, 1), 1, KMAX + 1)
    raw = jax.random.randint(key_raw, (H, NB), 0, KMAX)
    counts = 1 + raw % level
    full_at = jax.random.randint(key_full, (H, 1), 0, NB)
    column = jnp.arange(NB, dtype=jnp.int32)[None, :]
    return jnp.where(column == full_at, KMAX, counts).astype(jnp.int32)


def with_ends(drawn, stream_key, low, high):
    shape = drawn.shape
    spot = [jax.random.randint(jax.random.fold_in(stream_key, axis), (), 0, shape[axis]) for axis in range(len(shape))]
    drawn = drawn.at[tuple(spot)].set(low)
    longest = shape.index(max(shape))
    spot[longest] = (spot[longest] + 1) % shape[longest]
    return drawn.at[tuple(spot)].set(high)


def block_levels(rng, dims, shards, least, top_value):
    loudness = 1.0
    for axis_at, blocks in shards:
        heights = jax.random.uniform(jax.random.fold_in(jax.random.fold_in(rng, 6), axis_at), (blocks,), jnp.float32, least / len(shards), top_value / len(shards))
        loudness = loudness * jnp.repeat(jnp.exp(heights), dims[axis_at] // blocks).reshape((-1,) + (1,) * (len(dims) - 1 - axis_at))
    return loudness


def gaussian(stream_key, dims, spread, most, cuts=(), held_as=jnp.bfloat16):
    array = spread * jax.random.normal(stream_key, dims, jnp.float32)
    if cuts:
        array = array * block_levels(stream_key, dims, cuts, -0.22, 0.18)
    return jnp.clip(array, -most, most).astype(held_as)


def setup_inputs(seed: int = 0) -> dict:
    splits = jax.random.split(jax.random.key(seed), 9)
    queries = draw_queries(jax.random.fold_in(splits[8], 71), 0)
    keys = draw_keys(jax.random.fold_in(splits[8], 71), 0)
    values = gaussian(splits[2], (RECS, LEN, D), 1.0, 6.0, ((0, 8), (1, 16)))
    weight_out = gaussian(splits[3], (D, D), D ** -0.5, 0.125, ((0, 8),))
    cotangent = gaussian(splits[4], (RECS, LEN, D), 1.0, 6.0, ((0, 8), (1, 16)))
    hidden_mask = with_ends((jax.random.randint(splits[5], (RECS, LEN), 0, 2) < 1).astype(jnp.int32), jax.random.fold_in(splits[5], 1), 0, 1)
    pattern = draw_pattern(jax.random.fold_in(splits[8], 71), 0)
    live_slots = draw_live_slots(jax.random.fold_in(splits[8], 71), 0)
    return {"queries": queries, "keys": keys, "values": values, "weight_out": weight_out, "cotangent": cotangent, "hidden_mask": hidden_mask, "pattern": pattern, "live_slots": live_slots}


def block_scores(q_head, k_head, pat, live):
    scale = 1.0 / math.sqrt(HD)
    q_blocks = q_head.reshape(NB, BLOCK, HD).astype(jnp.float32)
    k_blocks = k_head.reshape(NB, BLOCK, HD).astype(jnp.float32)[pat].reshape(NB, KMAX * BLOCK, HD)
    scores = jnp.einsum('bid,bjd->bij', q_blocks, k_blocks) * scale
    slot_of = jnp.arange(KMAX * BLOCK, dtype=jnp.int32) // BLOCK
    valid = slot_of[None, :] < live[:, None]
    scores = jnp.where(valid[:, None, :], scores, jnp.float32(-1e+30))
    return (scores, q_blocks, k_blocks)

def forward_head(args):
    q_head, k_head, v_head, pat, live = args
    scores, q_blocks, k_blocks = block_scores(q_head, k_head, pat, live)
    v_blocks = v_head.reshape(NB, BLOCK, HD).astype(jnp.float32)[pat].reshape(NB, KMAX * BLOCK, HD)
    row_max = lax.optimization_barrier(jnp.max(scores, axis=-1))
    expo = jnp.exp(scores - row_max[..., None])
    row_sum = lax.optimization_barrier(jnp.sum(expo, axis=-1))
    probs = (expo / row_sum[..., None]).astype(jnp.bfloat16)
    attn = jnp.einsum('bij,bjd->bid', probs.astype(jnp.float32), v_blocks).astype(jnp.bfloat16)
    row_lse = row_max + jnp.log(row_sum)
    return (attn.reshape(LEN, HD), row_lse)

def backward_head(args):
    q_head, k_head, v_head, pat, live, attn, grad_attn, row_lse = args
    scale = 1.0 / math.sqrt(HD)
    scores, q_blocks, k_blocks = block_scores(q_head, k_head, pat, live)
    v_blocks = v_head.reshape(NB, BLOCK, HD).astype(jnp.float32)[pat].reshape(NB, KMAX * BLOCK, HD)
    d_blocks = grad_attn.reshape(NB, BLOCK, HD).astype(jnp.float32)
    a_blocks = attn.reshape(NB, BLOCK, HD).astype(jnp.float32)
    back_probs = jnp.exp(scores - row_lse[..., None])
    delta = lax.optimization_barrier(jnp.sum(d_blocks * a_blocks, axis=-1))
    dprobs = jnp.einsum('bid,bjd->bij', d_blocks, v_blocks)
    dscores = (back_probs * (dprobs - delta[..., None]) * scale).astype(jnp.bfloat16).astype(jnp.float32)
    probs_b = back_probs.astype(jnp.bfloat16).astype(jnp.float32)
    grad_q = jnp.einsum('bij,bjd->bid', dscores, k_blocks).astype(jnp.bfloat16)
    dk_parts = jnp.einsum('bij,bid->bjd', dscores, q_blocks).reshape(NB, KMAX, BLOCK, HD)
    dv_parts = jnp.einsum('bij,bid->bjd', probs_b, d_blocks).reshape(NB, KMAX, BLOCK, HD)
    grad_k = jnp.zeros((NB, BLOCK, HD), jnp.float32).at[pat].add(dk_parts).astype(jnp.bfloat16)
    grad_v = jnp.zeros((NB, BLOCK, HD), jnp.float32).at[pat].add(dv_parts).astype(jnp.bfloat16)
    return (grad_q.reshape(LEN, HD), grad_k.reshape(LEN, HD), grad_v.reshape(LEN, HD))

def split_heads(x):
    return x.reshape(RECS, LEN, H, HD).transpose(0, 2, 1, 3)

def merge_heads(x):
    return x.transpose(0, 2, 1, 3).reshape(RECS, LEN, H * HD)

def reference(queries, keys, values, weight_out, cotangent, hidden_mask, pattern, live_slots):
    q_all = split_heads(queries)
    k_all = split_heads(keys)
    v_all = split_heads(values)

    def forward_record(args):
        q_rec, k_rec, v_rec = args
        return lax.map(forward_head, (q_rec, k_rec, v_rec, pattern, live_slots))
    attn_heads, lse_heads = lax.map(forward_record, (q_all, k_all, v_all))
    attn = merge_heads(attn_heads)
    attn_flat = attn.reshape(RECS * LEN, H * HD)
    block_out = jnp.dot(attn_flat, weight_out, preferred_element_type=jnp.float32).astype(jnp.bfloat16)
    masked = cotangent * hidden_mask[..., None].astype(jnp.bfloat16)
    masked_flat = masked.reshape(RECS * LEN, H * HD)
    grad_attn = jnp.dot(masked_flat, weight_out.T, preferred_element_type=jnp.float32).astype(jnp.bfloat16)
    factor = 1.0 / math.sqrt(RECS * LEN)
    weight_grad = jnp.dot(attn_flat.T, masked_flat, preferred_element_type=jnp.float32) * factor
    grad_heads = split_heads(grad_attn.reshape(RECS, LEN, H * HD))

    def backward_record(args):
        q_rec, k_rec, v_rec, a_rec, g_rec, l_rec = args
        return lax.map(backward_head, (q_rec, k_rec, v_rec, pattern, live_slots, a_rec, g_rec, l_rec))
    grad_q, grad_k, grad_v = lax.map(backward_record, (q_all, k_all, v_all, attn_heads, grad_heads, lse_heads))
    return (block_out.reshape(RECS, LEN, H * HD), merge_heads(grad_q), merge_heads(grad_k), merge_heads(grad_v), weight_grad)
```

```python
import functools
import math

import jax
import jax.numpy as jnp
from jax import lax
from jax.experimental import pallas as pl
from jax.experimental.pallas import tpu as pltpu
from jax.sharding import PartitionSpec as P

HD = 128
BLOCK = 128
KMAX = 16
STEP = 4
SCALE = 1.0 / math.sqrt(HD)
BF = jnp.bfloat16
MESH = pl.DeviceIdType.MESH
NT = (((1,), (1,)), ((), ()))


def columns(index, width):
    return pl.ds(pl.multiple_of(index * width, width), width)


def greet(dp, seq, ndp, nseq):
    barrier = pltpu.get_barrier_semaphore()

    @pl.loop(1, nseq)
    def _(step):
        pl.semaphore_signal(barrier, inc=1, device_id=(dp, lax.rem(seq + step, nseq)), device_id_type=MESH)

    @pl.loop(1, ndp)
    def _(step):
        pl.semaphore_signal(barrier, inc=1, device_id=(lax.rem(dp + step, ndp), seq), device_id_type=MESH)

    pl.semaphore_wait(barrier, nseq + ndp - 2)


class Ring:
    def __init__(self, part, buf, dp, seq, ndp, send, recv, give, take):
        self.part, self.buf, self.dp, self.seq = part, buf, dp, seq
        self.chips = ndp // 2
        self.z, self.core = dp // 2, lax.rem(dp, 2)
        self.send, self.recv, self.give, self.take = send, recv, give, take

    def slot(self, offset, other=False):
        core = 1 - self.core if other else self.core
        return lax.rem(self.z + self.chips + offset, self.chips) * 2 + core

    def half(self, slot, half):
        return self.part(self.buf.at[slot], half)

    def hop(self, index, source=None):
        up = index % 2 == 0
        half = (0, 1, 1, 0, 0, 1)[index]
        slot = self.slot(0) if index < 4 else self.slot(-1 if up else 1)
        target = self.slot(1 if up else -1)
        src = self.half(slot, half) if source is None else self.part(source, half)
        return pltpu.make_async_remote_copy(src, self.half(slot, half), self.send.at[index], self.recv.at[index],
                                            device_id=(target, self.seq), device_id_type=MESH)

    def hand(self, index, source=None):
        if index < 2:
            slot, half = self.slot(0), index
        else:
            slot = self.slot((-1, 1, -1, 1, 2, 2)[index - 2])
            half = (0, 1, 1, 0, 0, 1)[index - 2]
        src = self.half(slot, half) if source is None else self.part(source, half)
        return pltpu.make_async_remote_copy(src, self.half(slot, half), self.give.at[index], self.take.at[index],
                                            device_id=(self.slot(0, True), self.seq), device_id_type=MESH)

    def start(self, half, source=None):
        for index in ((0, 3), (1, 2))[half]:
            self.hop(index, source).start()
        self.hand(half, source).start()

    def run(self, use):
        use(self.slot(0))
        for index in (0, 1):
            self.hop(index).wait_recv()
            self.hop(index + 4).start()
            self.hand(index + 2).start()
        self.hand(0).wait_recv()
        self.hand(1).wait_recv()
        use(self.slot(0, True))
        for index, offset in ((2, -1), (3, 1)):
            self.hop(index).wait_recv()
            self.hand(index + 2).start()
            use(self.slot(offset))
        for first, second, offset in ((2, 4, -1), (3, 5, 1)):
            self.hand(first).wait_recv()
            self.hand(second).wait_recv()
            use(self.slot(offset, True))
        for index in (4, 5):
            self.hop(index).wait_recv()
            self.hand(index + 2).start()
        use(self.slot(2))
        self.hand(6).wait_recv()
        self.hand(7).wait_recv()
        use(self.slot(2, True))
        for index in range(6):
            self.hop(index).wait_send()
        for index in range(8):
            self.hand(index).wait_send()


def bring(q_ref, k_ref, v_ref, w_ref, m_ref, hq_ref, hk_ref, hv_ref, hd_ref, wf_ref, mc_ref,
          w_buf, m_buf, g_buf, a_send, a_recv, w_send, w_recv, f_send, f_recv, m_send, m_recv, local, keep_w):
    dp, seq = lax.axis_index("dp"), lax.axis_index("seq")
    ndp, nseq = lax.axis_size("dp"), lax.axis_size("seq")
    rows, mine = w_ref.shape[0], q_ref.shape[0]
    tensors = ((q_ref, hq_ref), (k_ref, hk_ref), (v_ref, hv_ref))
    greet(dp, seq, ndp, nseq)

    def row_half(ref, half):
        return ref.at[pl.ds(half * (rows // 2), rows // 2), :]

    ring = Ring(row_half, w_buf, dp, seq, ndp, w_send, w_recv, f_send, f_recv)

    def sides(step):
        other = lax.rem(dp + step, ndp)
        return pltpu.make_async_remote_copy(m_ref.at[:, columns(other, rows)], mc_ref.at[dp], m_send.at[step], m_recv.at[step],
                                            device_id=(other, seq), device_id_type=MESH)

    def spread(which, step):
        src, dst = tensors[which]
        other = lax.rem(seq + step, nseq)
        return pltpu.make_async_remote_copy(src.at[:, columns(other, HD)], dst.at[columns(seq, mine), :],
                                            a_send.at[which, step], a_recv.at[which, step], device_id=(dp, other), device_id_type=MESH)

    def keep(which):
        src, dst = tensors[which]
        return pltpu.make_async_copy(src.at[:, columns(seq, HD)], dst.at[columns(seq, mine), :], local.at[which])

    own_w = pltpu.make_async_copy(w_ref, w_buf.at[dp], local.at[3])
    own_m = pltpu.make_async_copy(m_ref, m_buf, local.at[4])
    own_c = pltpu.make_async_copy(m_ref.at[:, columns(dp, rows)], mc_ref.at[dp], local.at[5])
    own_w.start()
    own_m.start()
    ring.start(0, w_ref)
    ring.start(1, w_ref)
    for which in range(3):
        @pl.loop(1, nseq)
        def _(step):
            spread(which, step).start()
        keep(which).start()
    own_c.start()

    @pl.loop(1, ndp)
    def _(step):
        sides(step).start()

    own_m.wait()

    def store(slot):
        return pltpu.make_async_copy(w_buf.at[slot], wf_ref.at[slot], keep_w.at[slot])

    def give(head, source):
        return pltpu.make_async_remote_copy(g_buf.at[:, columns(head, HD)], hd_ref.at[columns(source, mine), :],
                                            a_send.at[3, head], a_recv.at[3, source], device_id=(dp, head), device_id_type=MESH)

    def own_g():
        return pltpu.make_async_copy(g_buf.at[:, columns(seq, HD)], hd_ref.at[columns(seq, mine), :], local.at[6])

    def use(slot):
        store(slot).start()
        g_buf[:, columns(slot, rows)] = lax.dot_general(m_buf[...], w_buf[slot], NT, preferred_element_type=jnp.float32).astype(BF)
        for half in range(rows // HD):
            head = slot * (rows // HD) + half

            @pl.when(head != seq)
            def _():
                give(head, seq).start()

            @pl.when(head == seq)
            def _():
                own_g().start()

    own_w.wait()
    ring.run(use)
    own_c.wait()

    @pl.loop(1, ndp)
    def _(step):
        sides(step).wait()

    @pl.loop(0, ndp)
    def _(slot):
        store(slot).wait()

    for which in range(3):
        @pl.loop(1, nseq)
        def _(step):
            spread(which, step).wait()
        keep(which).wait()

    own_g().wait()

    @pl.loop(0, nseq)
    def _(other):
        @pl.when(other != seq)
        def _():
            give(other, seq).wait_send()
            give(other, other).wait_recv()


def bring_in(q, k, v, w, m):
    ndp, nseq = lax.axis_size("dp"), lax.axis_size("seq")
    mine, width = q.shape
    rows = w.shape[0]
    place = pl.BlockSpec(memory_space=pl.ANY)
    head = jax.ShapeDtypeStruct((mine * nseq, HD), BF)
    dma = pltpu.SemaphoreType.DMA
    return pl.pallas_call(
        bring,
        out_shape=(head,) * 4 + (jax.ShapeDtypeStruct((ndp, rows, width), BF), jax.ShapeDtypeStruct((ndp, mine, rows), BF)),
        in_specs=[place] * 5,
        out_specs=(place,) * 6,
        scratch_shapes=[
            pltpu.VMEM((ndp, rows, width), BF), pltpu.VMEM((mine, width), BF), pltpu.VMEM((mine, width), BF),
            dma((4, nseq)), dma((4, nseq)), dma((6,)), dma((6,)), dma((8,)), dma((8,)), dma((ndp,)), dma((ndp,)), dma((7,)), dma((ndp,))],
        compiler_params=pltpu.CompilerParams(collective_id=0, has_side_effects=True, vmem_limit_bytes=40 * 2**20),
        name="bring_in",
    )(q, k, v, w, m)


def take(factor, o_ref, dq_ref, dk_ref, dv_ref, wf_ref, mc_ref, out_ref, oq_ref, ok_ref, ov_ref, wg_ref,
         a_buf, w_buf, c_buf, ct_buf, sum_buf, p_buf, part_buf, out_buf, wg_buf,
         o_send, o_recv, g_send, g_recv, r_send, r_recv, f_send, f_recv, p_send, p_recv, local):
    dp, seq = lax.axis_index("dp"), lax.axis_index("seq")
    ndp, nseq = lax.axis_size("dp"), lax.axis_size("seq")
    mine, width = a_buf.shape[1:]
    rows = width // ndp
    tensors = ((dq_ref, oq_ref), (dk_ref, ok_ref), (dv_ref, ov_ref))
    greet(dp, seq, ndp, nseq)

    def column_half(ref, half):
        return ref.at[:, pl.ds(half * (width // 2), width // 2)]

    ring = Ring(column_half, a_buf, dp, seq, ndp, r_send, r_recv, f_send, f_recv)

    def home(other, source):
        return pltpu.make_async_remote_copy(o_ref.at[columns(other, mine), :], a_buf.at[dp].at[:, columns(source, HD)],
                                            o_send.at[other], o_recv.at[source], device_id=(dp, other), device_id_type=MESH)

    def spread(which, step):
        src, dst = tensors[which]
        other = lax.rem(seq + step, nseq)
        return pltpu.make_async_remote_copy(src.at[columns(other, mine), :], dst.at[:, columns(seq, HD)],
                                            g_send.at[which, step], g_recv.at[which, step], device_id=(dp, other), device_id_type=MESH)

    def keep(which):
        src, dst = tensors[which]
        return pltpu.make_async_copy(src.at[columns(seq, mine), :], dst.at[:, columns(seq, HD)], local.at[which])

    own_o = pltpu.make_async_copy(o_ref.at[columns(seq, mine), :], a_buf.at[dp].at[:, columns(seq, HD)], local.at[3])
    own_c = pltpu.make_async_copy(mc_ref, c_buf, local.at[4])
    own_w = pltpu.make_async_copy(wf_ref, w_buf, local.at[5])

    @pl.loop(1, nseq)
    def _(step):
        home(lax.rem(seq + step, nseq), seq).start()

    own_o.start()
    own_c.start()
    own_w.start()
    for which in range(3):
        @pl.loop(1, nseq)
        def _(step):
            spread(which, step).start()
        keep(which).start()

    own_c.wait()
    for slot in range(ndp):
        ct_buf[slot] = c_buf[slot].T
    sum_buf[...] = jnp.zeros_like(sum_buf)
    own_o.wait()
    for half in range(2):
        @pl.loop(half * (nseq // 2), (half + 1) * (nseq // 2))
        def _(other):
            @pl.when(other != seq)
            def _():
                home(other, other).wait_recv()
        ring.start(half)

    own_w.wait()

    @pl.loop(0, ndp)
    def _(tile):
        at = columns(tile, rows)
        total = jnp.zeros((mine, rows), jnp.float32)
        for slot in range(ndp):
            total += jnp.dot(a_buf[dp, :, slot * rows:(slot + 1) * rows], w_buf[slot, :, at], preferred_element_type=jnp.float32)
        out_buf[:, at] = total.astype(BF)

    own_out = pltpu.make_async_copy(out_buf, out_ref, local.at[6])
    own_out.start()

    def use(slot):
        @pl.loop(0, ndp)
        def _(tile):
            at = columns(tile, rows)
            sum_buf[:, at] += jnp.dot(ct_buf[slot], a_buf[slot, :, at], preferred_element_type=jnp.float32)

    ring.run(use)
    p_buf[...] = sum_buf[...].astype(BF)

    def share(head, source):
        return pltpu.make_async_remote_copy(p_buf.at[:, columns(head, HD)], part_buf.at[source],
                                            p_send.at[head], p_recv.at[source], device_id=(dp, head), device_id_type=MESH)

    own_p = pltpu.make_async_copy(p_buf.at[:, columns(seq, HD)], part_buf.at[seq], local.at[7])

    @pl.loop(1, nseq)
    def _(step):
        share(lax.rem(seq + step, nseq), seq).start()

    own_p.start()
    own_out.wait()
    for which in range(3):
        @pl.loop(1, nseq)
        def _(step):
            spread(which, step).wait()
        keep(which).wait()

    own_p.wait()

    @pl.loop(0, nseq)
    def _(other):
        @pl.when(other != seq)
        def _():
            home(other, seq).wait_send()
            share(other, seq).wait_send()
            share(other, other).wait_recv()

    total = part_buf[0].astype(jnp.float32)
    for source in range(1, nseq):
        total += part_buf[source].astype(jnp.float32)
    wg_buf[...] = total.T * factor
    last = pltpu.make_async_copy(wg_buf, wg_ref, local.at[8])
    last.start()
    last.wait()


def take_home(o, dq, dk, dv, wf, mc):
    ndp, nseq = lax.axis_size("dp"), lax.axis_size("seq")
    mine, rows = mc.shape[1:]
    width = rows * ndp
    place = pl.BlockSpec(memory_space=pl.ANY)
    out = jax.ShapeDtypeStruct((mine, width), BF)
    dma = pltpu.SemaphoreType.DMA
    factor = 1.0 / math.sqrt(ndp * nseq * mine)
    return pl.pallas_call(
        functools.partial(take, factor),
        out_shape=(out,) * 4 + (jax.ShapeDtypeStruct((HD, rows), jnp.float32),),
        in_specs=[place] * 6,
        out_specs=(place,) * 5,
        scratch_shapes=[
            pltpu.VMEM((ndp, mine, width), BF), pltpu.VMEM((ndp, rows, width), BF), pltpu.VMEM((ndp, mine, rows), BF),
            pltpu.VMEM((ndp, rows, mine), BF), pltpu.VMEM((rows, width), jnp.float32), pltpu.VMEM((rows, width), BF),
            pltpu.VMEM((nseq, rows, HD), BF), pltpu.VMEM((mine, width), BF), pltpu.VMEM((HD, rows), jnp.float32),
            dma((nseq,)), dma((nseq,)), dma((3, nseq)), dma((3, nseq)), dma((6,)), dma((6,)), dma((8,)), dma((8,)),
            dma((nseq,)), dma((nseq,)), dma((9,))],
        compiler_params=pltpu.CompilerParams(collective_id=1, has_side_effects=True, vmem_limit_bytes=48 * 2**20),
        name="take_home",
    )(o, dq, dk, dv, wf, mc)

def attend(step, pat_ref, live_ref, q_ref, k_ref, v_ref, d_ref, o_ref, dq_ref, dk_ref, dv_ref, kt_ref, vt_ref, acc_ref, e_ref, g_ref):
    nb = q_ref.shape[0] // BLOCK
    fold = lambda x: x.reshape(BLOCK // 8, 8, BLOCK)

    @pl.loop(0, nb)
    def _(b):
        rows = pl.ds(pl.multiple_of(b * BLOCK, BLOCK), BLOCK)
        kt_ref[rows, :] = k_ref[rows, :].T
        vt_ref[rows, :] = v_ref[rows, :].T
        acc_ref[rows, :] = jnp.zeros((BLOCK, 2 * HD), jnp.float32)

    def with_slots(count, b):
        rows = pl.ds(pl.multiple_of(b * BLOCK, BLOCK), BLOCK)
        live = live_ref[b]
        q = q_ref[rows, :]
        d = d_ref[rows, :]
        none = jnp.zeros((BLOCK, HD), BF)
        enter = jnp.concatenate([jnp.concatenate([q, none], 1), jnp.concatenate([none, d], 1)], 0)
        leave = jnp.concatenate([jnp.concatenate([d, none], 1), jnp.concatenate([none, q], 1)], 0)
        at = [pl.ds(pl.multiple_of(pat_ref[b * KMAX + j] * BLOCK, BLOCK), BLOCK) for j in range(count)]
        top = jnp.full((8, BLOCK), -1e30, jnp.float32)
        total = jnp.zeros((8, BLOCK), jnp.float32)
        mixed = jnp.zeros((8, BLOCK), jnp.float32)
        tops = []
        for j in range(count):
            both = lax.dot_general(jnp.concatenate([k_ref[at[j], :], v_ref[at[j], :]], 1), enter,
                                   (((1,), (1,)), ((), ())), preferred_element_type=jnp.float32)
            s, g = both[:, :BLOCK], both[:, BLOCK:]
            if j > count - step:
                s = jnp.where(j < live, s, jnp.float32(-1e30))
            new = jnp.maximum(top, jnp.max(fold(s), axis=0))
            old = jnp.exp((top - new) * SCALE)
            e = jnp.exp((fold(s) - new[None]) * SCALE)
            total = total * old + jnp.sum(e, axis=0)
            mixed = mixed * old + jnp.sum(e * fold(g), axis=0)
            e_ref[j * BLOCK:(j + 1) * BLOCK, :] = e.reshape(BLOCK, BLOCK)
            g_ref[j * BLOCK:(j + 1) * BLOCK, :] = g
            tops.append(new)
            top = new
        peak = jnp.max(top, axis=0, keepdims=True)
        level = jnp.exp((top - peak) * SCALE)
        inverse = 1.0 / jnp.sum(total * level, axis=0, keepdims=True)
        delta = jnp.sum(mixed * level, axis=0, keepdims=True) * inverse
        o_sum = jnp.zeros((HD, BLOCK), jnp.float32)
        q_sum = jnp.zeros((HD, BLOCK), jnp.float32)
        for j in range(0, count, 2):
            probs, slopes = [], []
            for i in (j, j + 1):
                e = e_ref[i * BLOCK:(i + 1) * BLOCK, :]
                g = g_ref[i * BLOCK:(i + 1) * BLOCK, :]
                weight = jnp.exp((tops[i] - peak) * SCALE) * inverse
                p = (fold(e) * weight[None]).reshape(BLOCK, BLOCK)
                pb = p.astype(BF)
                sb = (p * (g - delta)).astype(BF)
                acc_ref[at[i], :] += jnp.dot(jnp.concatenate([pb, sb], 1), leave, preferred_element_type=jnp.float32)
                probs.append(pb)
                slopes.append(sb)
            o_sum += jnp.dot(jnp.concatenate([vt_ref[at[j], :], vt_ref[at[j + 1], :]], 1),
                             jnp.concatenate(probs, 0), preferred_element_type=jnp.float32)
            q_sum += jnp.dot(jnp.concatenate([kt_ref[at[j], :], kt_ref[at[j + 1], :]], 1),
                             jnp.concatenate(slopes, 0), preferred_element_type=jnp.float32)
        o_ref[rows, :] = o_sum.T.astype(BF)
        dq_ref[rows, :] = (q_sum.T * SCALE).astype(BF)

    @pl.loop(0, nb)
    def _(b):
        branches = [functools.partial(with_slots, c) for c in range(step, KMAX + 1, step)]
        lax.switch((live_ref[b] - 1) // step, branches, b)

    @pl.loop(0, nb)
    def _(b):
        rows = pl.ds(pl.multiple_of(b * BLOCK, BLOCK), BLOCK)
        dv_ref[rows, :] = acc_ref[rows, :HD].astype(BF)
        dk_ref[rows, :] = (acc_ref[rows, HD:] * SCALE).astype(BF)


def attention(q, k, v, d, pat, live):
    length = q.shape[0]
    out = jax.ShapeDtypeStruct((length, HD), BF)
    vm = pl.BlockSpec(memory_space=pltpu.VMEM)
    sm = pl.BlockSpec(memory_space=pltpu.SMEM)
    return pl.pallas_call(
        functools.partial(attend, STEP),
        out_shape=(out,) * 4,
        in_specs=[sm, sm, vm, vm, vm, vm],
        out_specs=(vm,) * 4,
        scratch_shapes=[
            pltpu.VMEM((length, HD), BF), pltpu.VMEM((length, HD), BF),
            pltpu.VMEM((length, 2 * HD), jnp.float32),
            pltpu.VMEM((KMAX * BLOCK, BLOCK), jnp.float32), pltpu.VMEM((KMAX * BLOCK, BLOCK), jnp.float32)],
        compiler_params=pltpu.CompilerParams(vmem_limit_bytes=40 * 2**20),
        name="attention",
    )(pat.reshape(-1), live, q, k, v, d)


def local(queries, keys, values, weight_out, cotangent, hidden_mask, pattern, live_slots):
    seq = lax.axis_index("seq")
    pat = lax.dynamic_index_in_dim(pattern, seq, 0, keepdims=False)
    live = lax.dynamic_index_in_dim(live_slots, seq, 0, keepdims=False)
    masked = cotangent[0] * hidden_mask[0][:, None].astype(BF)
    q, k, v, d, weights, sides = bring_in(queries[0], keys[0], values[0], weight_out, masked)
    attn, dq, dk, dv = attention(q, k, v, d, pat, live)
    block_out, dq, dk, dv, weight_grad = take_home(attn, dq, dk, dv, weights, sides)
    return (block_out[None], dq[None], dk[None], dv[None], weight_grad)


def solution(mesh):
    rows = P("dp", "seq", None)
    return jax.shard_map(
        local,
        mesh=mesh,
        in_specs=(rows, rows, rows, P("dp", None), rows, P("dp", "seq"), P(), P()),
        out_specs=(rows, rows, rows, rows, P("seq", "dp")),
        check_vma=False,
    )
```

```python
import functools
import math

import jax
import jax.numpy as jnp
from jax import lax
from jax.experimental import pallas as pl
from jax.experimental.pallas import tpu as pltpu
from jax.sharding import PartitionSpec as P

HD = 128
BLOCK = 128
KMAX = 16
STEP = 4
SCALE = 1.0 / math.sqrt(HD)
BF = jnp.bfloat16
MESH = pl.DeviceIdType.MESH
NT = (((1,), (1,)), ((), ()))


def columns(index, width):
    return pl.ds(pl.multiple_of(index * width, width), width)


def greet(dp, seq, ndp, nseq):
    barrier = pltpu.get_barrier_semaphore()

    @pl.loop(1, nseq)
    def _(step):
        pl.semaphore_signal(barrier, inc=1, device_id=(dp, lax.rem(seq + step, nseq)), device_id_type=MESH)

    @pl.loop(1, ndp)
    def _(step):
        pl.semaphore_signal(barrier, inc=1, device_id=(lax.rem(dp + step, ndp), seq), device_id_type=MESH)

    pl.semaphore_wait(barrier, nseq + ndp - 2)


class Ring:
    def __init__(self, part, buf, dp, seq, ndp, send, recv, give, take):
        self.part, self.buf, self.dp, self.seq = part, buf, dp, seq
        self.chips = ndp // 2
        self.z, self.core = dp // 2, lax.rem(dp, 2)
        self.send, self.recv, self.give, self.take = send, recv, give, take

    def slot(self, offset, other=False):
        core = 1 - self.core if other else self.core
        return lax.rem(self.z + self.chips + offset, self.chips) * 2 + core

    def half(self, slot, half):
        return self.part(self.buf.at[slot], half)

    def hop(self, index, source=None):
        up = index % 2 == 0
        half = (0, 1, 1, 0, 0, 1)[index]
        slot = self.slot(0) if index < 4 else self.slot(-1 if up else 1)
        target = self.slot(1 if up else -1)
        src = self.half(slot, half) if source is None else self.part(source, half)
        return pltpu.make_async_remote_copy(src, self.half(slot, half), self.send.at[index], self.recv.at[index],
                                            device_id=(target, self.seq), device_id_type=MESH)

    def hand(self, index, source=None):
        if index < 2:
            slot, half = self.slot(0), index
        else:
            slot = self.slot((-1, 1, -1, 1, 2, 2)[index - 2])
            half = (0, 1, 1, 0, 0, 1)[index - 2]
        src = self.half(slot, half) if source is None else self.part(source, half)
        return pltpu.make_async_remote_copy(src, self.half(slot, half), self.give.at[index], self.take.at[index],
                                            device_id=(self.slot(0, True), self.seq), device_id_type=MESH)

    def start(self, half, source=None):
        for index in ((0, 3), (1, 2))[half]:
            self.hop(index, source).start()
        self.hand(half, source).start()

    def run(self, use):
        use(self.slot(0))
        for index in (0, 1):
            self.hop(index).wait_recv()
            self.hop(index + 4).start()
            self.hand(index + 2).start()
        self.hand(0).wait_recv()
        self.hand(1).wait_recv()
        use(self.slot(0, True))
        for index, offset in ((2, -1), (3, 1)):
            self.hop(index).wait_recv()
            self.hand(index + 2).start()
            use(self.slot(offset))
        for first, second, offset in ((2, 4, -1), (3, 5, 1)):
            self.hand(first).wait_recv()
            self.hand(second).wait_recv()
            use(self.slot(offset, True))
        for index in (4, 5):
            self.hop(index).wait_recv()
            self.hand(index + 2).start()
        use(self.slot(2))
        self.hand(6).wait_recv()
        self.hand(7).wait_recv()
        use(self.slot(2, True))
        for index in range(6):
            self.hop(index).wait_send()
        for index in range(8):
            self.hand(index).wait_send()


def bring(q_ref, k_ref, v_ref, w_ref, m_ref, hq_ref, hk_ref, hv_ref, hd_ref, wf_ref, mc_ref,
          w_buf, m_buf, g_buf, a_send, a_recv, w_send, w_recv, f_send, f_recv, m_send, m_recv, local, keep_w):
    dp, seq = lax.axis_index("dp"), lax.axis_index("seq")
    ndp, nseq = lax.axis_size("dp"), lax.axis_size("seq")
    rows, mine = w_ref.shape[0], q_ref.shape[0]
    tensors = ((q_ref, hq_ref), (k_ref, hk_ref), (v_ref, hv_ref))
    greet(dp, seq, ndp, nseq)

    def row_half(ref, half):
        return ref.at[pl.ds(half * (rows // 2), rows // 2), :]

    ring = Ring(row_half, w_buf, dp, seq, ndp, w_send, w_recv, f_send, f_recv)

    def sides(step):
        other = lax.rem(dp + step, ndp)
        return pltpu.make_async_remote_copy(m_ref.at[:, columns(other, rows)], mc_ref.at[dp], m_send.at[step], m_recv.at[step],
                                            device_id=(other, seq), device_id_type=MESH)

    def spread(which, step):
        src, dst = tensors[which]
        other = lax.rem(seq + step, nseq)
        return pltpu.make_async_remote_copy(src.at[:, columns(other, HD)], dst.at[columns(seq, mine), :],
                                            a_send.at[which, step], a_recv.at[which, step], device_id=(dp, other), device_id_type=MESH)

    def keep(which):
        src, dst = tensors[which]
        return pltpu.make_async_copy(src.at[:, columns(seq, HD)], dst.at[columns(seq, mine), :], local.at[which])

    own_w = pltpu.make_async_copy(w_ref, w_buf.at[dp], local.at[3])
    own_m = pltpu.make_async_copy(m_ref, m_buf, local.at[4])
    own_c = pltpu.make_async_copy(m_ref.at[:, columns(dp, rows)], mc_ref.at[dp], local.at[5])
    own_w.start()
    own_m.start()
    ring.start(0, w_ref)
    ring.start(1, w_ref)
    for which in range(3):
        @pl.loop(1, nseq)
        def _(step):
            spread(which, step).start()
        keep(which).start()
    own_c.start()

    @pl.loop(1, ndp)
    def _(step):
        sides(step).start()

    own_m.wait()

    def store(slot):
        return pltpu.make_async_copy(w_buf.at[slot], wf_ref.at[slot], keep_w.at[slot])

    def give(head, source):
        return pltpu.make_async_remote_copy(g_buf.at[:, columns(head, HD)], hd_ref.at[columns(source, mine), :],
                                            a_send.at[3, head], a_recv.at[3, source], device_id=(dp, head), device_id_type=MESH)

    def own_g():
        return pltpu.make_async_copy(g_buf.at[:, columns(seq, HD)], hd_ref.at[columns(seq, mine), :], local.at[6])

    def use(slot):
        store(slot).start()
        g_buf[:, columns(slot, rows)] = lax.dot_general(m_buf[...], w_buf[slot], NT, preferred_element_type=jnp.float32).astype(BF)
        for half in range(rows // HD):
            head = slot * (rows // HD) + half

            @pl.when(head != seq)
            def _():
                give(head, seq).start()

            @pl.when(head == seq)
            def _():
                own_g().start()

    own_w.wait()
    ring.run(use)
    own_c.wait()

    @pl.loop(1, ndp)
    def _(step):
        sides(step).wait()

    @pl.loop(0, ndp)
    def _(slot):
        store(slot).wait()

    for which in range(3):
        @pl.loop(1, nseq)
        def _(step):
            spread(which, step).wait()
        keep(which).wait()

    own_g().wait()

    @pl.loop(0, nseq)
    def _(other):
        @pl.when(other != seq)
        def _():
            give(other, seq).wait_send()
            give(other, other).wait_recv()


def bring_in(q, k, v, w, m):
    ndp, nseq = lax.axis_size("dp"), lax.axis_size("seq")
    mine, width = q.shape
    rows = w.shape[0]
    place = pl.BlockSpec(memory_space=pl.ANY)
    head = jax.ShapeDtypeStruct((mine * nseq, HD), BF)
    dma = pltpu.SemaphoreType.DMA
    return pl.pallas_call(
        bring,
        out_shape=(head,) * 4 + (jax.ShapeDtypeStruct((ndp, rows, width), BF), jax.ShapeDtypeStruct((ndp, mine, rows), BF)),
        in_specs=[place] * 5,
        out_specs=(place,) * 6,
        scratch_shapes=[
            pltpu.VMEM((ndp, rows, width), BF), pltpu.VMEM((mine, width), BF), pltpu.VMEM((mine, width), BF),
            dma((4, nseq)), dma((4, nseq)), dma((6,)), dma((6,)), dma((8,)), dma((8,)), dma((ndp,)), dma((ndp,)), dma((7,)), dma((ndp,))],
        compiler_params=pltpu.CompilerParams(collective_id=0, has_side_effects=True, vmem_limit_bytes=60 * 2**20),
        name="bring_in",
    )(q, k, v, w, m)


def take(factor, o_ref, dq_ref, dk_ref, dv_ref, wf_ref, mc_ref, out_ref, oq_ref, ok_ref, ov_ref, wg_ref,
         a_buf, w_buf, c_buf, ct_buf, p_buf, part_buf, out_buf, wg_buf,
         o_send, o_recv, g_send, g_recv, r_send, r_recv, f_send, f_recv, p_send, p_recv, local):
    dp, seq = lax.axis_index("dp"), lax.axis_index("seq")
    ndp, nseq = lax.axis_size("dp"), lax.axis_size("seq")
    chips = ndp // 2
    z, core = dp // 2, lax.rem(dp, 2)
    mine, width = a_buf.shape[1:]
    rows = width // ndp
    tensors = ((dq_ref, oq_ref), (dk_ref, ok_ref), (dv_ref, ov_ref))
    greet(dp, seq, ndp, nseq)

    def slot(offset, other=False):
        return lax.rem(z + chips + offset, chips) * 2 + (1 - core if other else core)

    def head_at(step):
        return lax.rem(seq + nseq - step, nseq)

    def home(other, source):
        return pltpu.make_async_remote_copy(o_ref.at[columns(other, mine), :], a_buf.at[dp].at[:, columns(source, HD)],
                                            o_send.at[other], o_recv.at[source], device_id=(dp, other), device_id_type=MESH)

    def hop(kind, step):
        way = (1, -1, 1 - 2 * lax.rem(step, 2))[kind]
        origin = slot(0) if kind < 2 else slot(-way)
        piece = a_buf.at[origin].at[:, columns(head_at(step), HD)]
        return pltpu.make_async_remote_copy(piece, piece, r_send.at[kind, step], r_recv.at[kind, step],
                                            device_id=(slot(way), seq), device_id_type=MESH)

    def hand(kind, step):
        piece = a_buf.at[slot((0, -1, 1, 2)[kind])].at[:, columns(head_at(step), HD)]
        return pltpu.make_async_remote_copy(piece, piece, f_send.at[kind, step], f_recv.at[kind, step],
                                            device_id=(slot(0, True), seq), device_id_type=MESH)

    def spread(which, step):
        src, dst = tensors[which]
        other = lax.rem(seq + step, nseq)
        return pltpu.make_async_remote_copy(src.at[columns(other, mine), :], dst.at[:, columns(seq, HD)],
                                            g_send.at[which, step], g_recv.at[which, step], device_id=(dp, other), device_id_type=MESH)

    def keep(which):
        src, dst = tensors[which]
        return pltpu.make_async_copy(src.at[columns(seq, mine), :], dst.at[:, columns(seq, HD)], local.at[which])

    def share(head, source):
        return pltpu.make_async_remote_copy(p_buf.at[:, columns(head, HD)], part_buf.at[source],
                                            p_send.at[head], p_recv.at[source], device_id=(dp, head), device_id_type=MESH)

    own_p = pltpu.make_async_copy(p_buf.at[:, columns(seq, HD)], part_buf.at[seq], local.at[7])
    own_o = pltpu.make_async_copy(o_ref.at[columns(seq, mine), :], a_buf.at[dp].at[:, columns(seq, HD)], local.at[3])
    own_c = pltpu.make_async_copy(mc_ref, c_buf, local.at[4])
    own_w = pltpu.make_async_copy(wf_ref, w_buf, local.at[5])
    own_out = pltpu.make_async_copy(out_buf, out_ref, local.at[6])
    own_o.start()

    @pl.loop(1, nseq)
    def _(step):
        home(lax.rem(seq + step, nseq), seq).start()

    own_c.start()
    own_w.start()
    for which in range(3):
        @pl.loop(1, nseq)
        def _(step):
            spread(which, step).start()
        keep(which).start()

    own_c.wait()
    for source in range(ndp):
        ct_buf[:, source * mine:(source + 1) * mine] = c_buf[source].T
    own_o.wait()

    @pl.loop(0, nseq + 3)
    def _(turn):
        @pl.when(turn < nseq)
        def _():
            @pl.when(turn > 0)
            def _():
                home(head_at(turn), head_at(turn)).wait_recv()
            hop(0, turn).start()
            hop(1, turn).start()
            hand(0, turn).start()

        @pl.when((turn >= 1) & (turn < nseq + 1))
        def _():
            step = turn - 1
            hop(0, step).wait_recv()
            hop(1, step).wait_recv()
            hop(2, step).start()
            hand(1, step).start()
            hand(2, step).start()

        @pl.when((turn >= 2) & (turn < nseq + 2))
        def _():
            step = turn - 2
            hop(2, step).wait_recv()
            hand(3, step).start()

        @pl.when(turn >= 3)
        def _():
            step = turn - 3
            for kind in range(4):
                hand(kind, step).wait_recv()
            at = columns(head_at(step), HD)
            pieces = a_buf[:, :, at].reshape(ndp * mine, HD)
            p_buf[:, at] = jnp.dot(ct_buf[...], pieces, preferred_element_type=jnp.float32).astype(BF)

            @pl.when(step > 0)
            def _():
                share(head_at(step), seq).start()

            @pl.when(step == 0)
            def _():
                own_p.start()

    own_w.wait()

    @pl.loop(0, ndp)
    def _(tile):
        at = columns(tile, rows)
        total = jnp.zeros((mine, rows), jnp.float32)
        for source in range(ndp):
            total += jnp.dot(a_buf[dp, :, source * rows:(source + 1) * rows], w_buf[source, :, at], preferred_element_type=jnp.float32)
        out_buf[:, at] = total.astype(BF)

    own_out.start()
    own_p.wait()
    wg_buf[...] = part_buf[seq].astype(jnp.float32)

    @pl.loop(1, nseq)
    def _(step):
        source = lax.rem(seq + step, nseq)
        share(source, source).wait_recv()
        wg_buf[...] += part_buf[source].astype(jnp.float32)

    wg_ref[...] = wg_buf[...].T * factor
    for which in range(3):
        @pl.loop(1, nseq)
        def _(step):
            spread(which, step).wait()
        keep(which).wait()

    @pl.loop(0, nseq)
    def _(step):
        @pl.when(step > 0)
        def _():
            home(head_at(step), seq).wait_send()
            share(head_at(step), seq).wait_send()
        for kind in range(3):
            hop(kind, step).wait_send()
        for kind in range(4):
            hand(kind, step).wait_send()
    own_out.wait()


def take_home(o, dq, dk, dv, wf, mc):
    ndp, nseq = lax.axis_size("dp"), lax.axis_size("seq")
    mine, rows = mc.shape[1:]
    width = rows * ndp
    place = pl.BlockSpec(memory_space=pl.ANY)
    out = jax.ShapeDtypeStruct((mine, width), BF)
    dma = pltpu.SemaphoreType.DMA
    factor = 1.0 / math.sqrt(ndp * nseq * mine)
    return pl.pallas_call(
        functools.partial(take, factor),
        out_shape=(out,) * 4 + (jax.ShapeDtypeStruct((HD, rows), jnp.float32),),
        in_specs=[place] * 6,
        out_specs=(place,) * 4 + (pl.BlockSpec(memory_space=pltpu.VMEM),),
        scratch_shapes=[
            pltpu.VMEM((ndp, mine, width), BF), pltpu.VMEM((ndp, rows, width), BF), pltpu.VMEM((ndp, mine, rows), BF),
            pltpu.VMEM((rows, ndp * mine), BF), pltpu.VMEM((rows, width), BF),
            pltpu.VMEM((nseq, rows, HD), BF), pltpu.VMEM((mine, width), BF), pltpu.VMEM((rows, HD), jnp.float32),
            dma((nseq,)), dma((nseq,)), dma((3, nseq)), dma((3, nseq)), dma((3, nseq)), dma((3, nseq)), dma((4, nseq)), dma((4, nseq)),
            dma((nseq,)), dma((nseq,)), dma((8,))],
        compiler_params=pltpu.CompilerParams(collective_id=1, has_side_effects=True, vmem_limit_bytes=60 * 2**20),
        name="take_home",
    )(o, dq, dk, dv, wf, mc)

def attend(step, pat_ref, live_ref, q_ref, k_ref, v_ref, d_ref, o_ref, dq_ref, dk_ref, dv_ref, kt_ref, vt_ref, acc_ref, e_ref, g_ref):
    nb = q_ref.shape[0] // BLOCK
    fold = lambda x: x.reshape(BLOCK // 8, 8, BLOCK)

    @pl.loop(0, nb)
    def _(b):
        rows = pl.ds(pl.multiple_of(b * BLOCK, BLOCK), BLOCK)
        kt_ref[rows, :] = k_ref[rows, :].T
        vt_ref[rows, :] = v_ref[rows, :].T
        acc_ref[rows, :] = jnp.zeros((BLOCK, 2 * HD), jnp.float32)

    def with_slots(count, b):
        rows = pl.ds(pl.multiple_of(b * BLOCK, BLOCK), BLOCK)
        live = live_ref[b]
        q = q_ref[rows, :]
        d = d_ref[rows, :]
        none = jnp.zeros((BLOCK, HD), BF)
        enter = jnp.concatenate([jnp.concatenate([q, none], 1), jnp.concatenate([none, d], 1)], 0)
        leave = jnp.concatenate([jnp.concatenate([d, none], 1), jnp.concatenate([none, q], 1)], 0)
        at = [pl.ds(pl.multiple_of(pat_ref[b * KMAX + j] * BLOCK, BLOCK), BLOCK) for j in range(count)]
        top = jnp.full((8, BLOCK), -1e30, jnp.float32)
        total = jnp.zeros((8, BLOCK), jnp.float32)
        mixed = jnp.zeros((8, BLOCK), jnp.float32)
        tops = []
        for j in range(count):
            both = lax.dot_general(jnp.concatenate([k_ref[at[j], :], v_ref[at[j], :]], 1), enter,
                                   (((1,), (1,)), ((), ())), preferred_element_type=jnp.float32)
            s, g = both[:, :BLOCK], both[:, BLOCK:]
            if j > count - step:
                s = jnp.where(j < live, s, jnp.float32(-1e30))
            new = jnp.maximum(top, jnp.max(fold(s), axis=0))
            old = jnp.exp((top - new) * SCALE)
            e = jnp.exp((fold(s) - new[None]) * SCALE)
            total = total * old + jnp.sum(e, axis=0)
            mixed = mixed * old + jnp.sum(e * fold(g), axis=0)
            e_ref[j * BLOCK:(j + 1) * BLOCK, :] = e.reshape(BLOCK, BLOCK)
            g_ref[j * BLOCK:(j + 1) * BLOCK, :] = g
            tops.append(new)
            top = new
        peak = jnp.max(top, axis=0, keepdims=True)
        level = jnp.exp((top - peak) * SCALE)
        inverse = 1.0 / jnp.sum(total * level, axis=0, keepdims=True)
        delta = jnp.sum(mixed * level, axis=0, keepdims=True) * inverse
        o_sum = jnp.zeros((HD, BLOCK), jnp.float32)
        q_sum = jnp.zeros((HD, BLOCK), jnp.float32)
        for j in range(0, count, 2):
            probs, slopes = [], []
            for i in (j, j + 1):
                e = e_ref[i * BLOCK:(i + 1) * BLOCK, :]
                g = g_ref[i * BLOCK:(i + 1) * BLOCK, :]
                weight = jnp.exp((tops[i] - peak) * SCALE) * inverse
                p = (fold(e) * weight[None]).reshape(BLOCK, BLOCK)
                pb = p.astype(BF)
                sb = (p * (g - delta)).astype(BF)
                acc_ref[at[i], :] += jnp.dot(jnp.concatenate([pb, sb], 1), leave, preferred_element_type=jnp.float32)
                probs.append(pb)
                slopes.append(sb)
            o_sum += jnp.dot(jnp.concatenate([vt_ref[at[j], :], vt_ref[at[j + 1], :]], 1),
                             jnp.concatenate(probs, 0), preferred_element_type=jnp.float32)
            q_sum += jnp.dot(jnp.concatenate([kt_ref[at[j], :], kt_ref[at[j + 1], :]], 1),
                             jnp.concatenate(slopes, 0), preferred_element_type=jnp.float32)
        o_ref[rows, :] = o_sum.T.astype(BF)
        dq_ref[rows, :] = (q_sum.T * SCALE).astype(BF)

    @pl.loop(0, nb)
    def _(b):
        branches = [functools.partial(with_slots, c) for c in range(step, KMAX + 1, step)]
        lax.switch((live_ref[b] - 1) // step, branches, b)

    @pl.loop(0, nb)
    def _(b):
        rows = pl.ds(pl.multiple_of(b * BLOCK, BLOCK), BLOCK)
        dv_ref[rows, :] = acc_ref[rows, :HD].astype(BF)
        dk_ref[rows, :] = (acc_ref[rows, HD:] * SCALE).astype(BF)


def attention(q, k, v, d, pat, live):
    length = q.shape[0]
    out = jax.ShapeDtypeStruct((length, HD), BF)
    vm = pl.BlockSpec(memory_space=pltpu.VMEM)
    sm = pl.BlockSpec(memory_space=pltpu.SMEM)
    return pl.pallas_call(
        functools.partial(attend, STEP),
        out_shape=(out,) * 4,
        in_specs=[sm, sm, vm, vm, vm, vm],
        out_specs=(vm,) * 4,
        scratch_shapes=[
            pltpu.VMEM((length, HD), BF), pltpu.VMEM((length, HD), BF),
            pltpu.VMEM((length, 2 * HD), jnp.float32),
            pltpu.VMEM((KMAX * BLOCK, BLOCK), jnp.float32), pltpu.VMEM((KMAX * BLOCK, BLOCK), jnp.float32)],
        compiler_params=pltpu.CompilerParams(vmem_limit_bytes=60 * 2**20),
        name="attention",
    )(pat.reshape(-1), live, q, k, v, d)


def local(queries, keys, values, weight_out, cotangent, hidden_mask, pattern, live_slots):
    seq = lax.axis_index("seq")
    pat = lax.dynamic_index_in_dim(pattern, seq, 0, keepdims=False)
    live = lax.dynamic_index_in_dim(live_slots, seq, 0, keepdims=False)
    masked = cotangent[0] * hidden_mask[0][:, None].astype(BF)
    q, k, v, d, weights, sides = bring_in(queries[0], keys[0], values[0], weight_out, masked)
    attn, dq, dk, dv = attention(q, k, v, d, pat, live)
    block_out, dq, dk, dv, weight_grad = take_home(attn, dq, dk, dv, weights, sides)
    return (block_out[None], dq[None], dk[None], dv[None], weight_grad)


def solution(mesh):
    rows = P("dp", "seq", None)
    return jax.shard_map(
        local,
        mesh=mesh,
        in_specs=(rows, rows, rows, P("dp", None), rows, P("dp", "seq"), P(), P()),
        out_specs=(rows, rows, rows, rows, P("seq", "dp")),
        check_vma=False,
    )
```

```python
import functools
import math

import jax
import jax.numpy as jnp
from jax import lax
from jax.experimental import pallas as pl
from jax.experimental.pallas import tpu as pltpu
from jax.sharding import PartitionSpec as P

HD = 128
BLOCK = 128
KMAX = 16
STEP = 2
GROUP = 2
PAIR = 4
UNROLL = 4
SCALE = 1.0 / math.sqrt(HD)
BF = jnp.bfloat16
MESH = pl.DeviceIdType.MESH
NT = (((1,), (1,)), ((), ()))


def columns(index, width):
    return pl.ds(pl.multiple_of(index * width, width), width)


def greet(dp, seq, ndp, nseq):
    barrier = pltpu.get_barrier_semaphore()

    @pl.loop(1, nseq)
    def _(step):
        pl.semaphore_signal(barrier, inc=1, device_id=(dp, lax.rem(seq + step, nseq)), device_id_type=MESH)

    @pl.loop(1, ndp)
    def _(step):
        pl.semaphore_signal(barrier, inc=1, device_id=(lax.rem(dp + step, ndp), seq), device_id_type=MESH)

    pl.semaphore_wait(barrier, nseq + ndp - 2)


class Ring:
    def __init__(self, part, buf, dp, seq, ndp, send, recv, give, take):
        self.part, self.buf, self.dp, self.seq = part, buf, dp, seq
        self.chips = ndp // 2
        self.z, self.core = dp // 2, lax.rem(dp, 2)
        self.send, self.recv, self.give, self.take = send, recv, give, take

    def slot(self, offset, other=False):
        core = 1 - self.core if other else self.core
        return lax.rem(self.z + self.chips + offset, self.chips) * 2 + core

    def half(self, slot, half):
        return self.part(self.buf.at[slot], half)

    def hop(self, index, source=None):
        up = index % 2 == 0
        half = (0, 1, 1, 0, 0, 1)[index]
        slot = self.slot(0) if index < 4 else self.slot(-1 if up else 1)
        target = self.slot(1 if up else -1)
        src = self.half(slot, half) if source is None else self.part(source, half)
        return pltpu.make_async_remote_copy(src, self.half(slot, half), self.send.at[index], self.recv.at[index],
                                            device_id=(target, self.seq), device_id_type=MESH)

    def hand(self, index, source=None):
        if index < 2:
            slot, half = self.slot(0), index
        else:
            slot = self.slot((-1, 1, -1, 1, 2, 2)[index - 2])
            half = (0, 1, 1, 0, 0, 1)[index - 2]
        src = self.half(slot, half) if source is None else self.part(source, half)
        return pltpu.make_async_remote_copy(src, self.half(slot, half), self.give.at[index], self.take.at[index],
                                            device_id=(self.slot(0, True), self.seq), device_id_type=MESH)

    def start(self, half, source=None):
        for index in ((0, 3), (1, 2))[half]:
            self.hop(index, source).start()
        self.hand(half, source).start()

    def run(self, use, late):
        use(self.slot(0))
        for index in (0, 1):
            self.hop(index).wait_recv()
            self.hop(index + 4).start()
            self.hand(index + 2).start()
        self.hand(0).wait_recv()
        self.hand(1).wait_recv()
        use(self.slot(0, True))
        for index, offset in ((2, -1), (3, 1)):
            self.hop(index).wait_recv()
            self.hand(index + 2).start()
            use(self.slot(offset))
        for first, second, offset in ((2, 4, -1), (3, 5, 1)):
            self.hand(first).wait_recv()
            self.hand(second).wait_recv()
            use(self.slot(offset, True))
        for index in (4, 5):
            self.hop(index).wait_recv()
            self.hand(index + 2).start()
        late()
        use(self.slot(2))
        self.hand(6).wait_recv()
        self.hand(7).wait_recv()
        use(self.slot(2, True))
        for index in range(6):
            self.hop(index).wait_send()
        for index in range(8):
            self.hand(index).wait_send()


def bring(mask_ref, q_ref, k_ref, v_ref, w_ref, m_ref, hq_ref, hk_ref, hv_ref, hd_ref, wf_ref, mc_ref,
          w_buf, m_buf, g_buf, a_send, a_recv, w_send, w_recv, f_send, f_recv, m_send, m_recv, local, keep_w):
    dp, seq = lax.axis_index("dp"), lax.axis_index("seq")
    ndp, nseq = lax.axis_size("dp"), lax.axis_size("seq")
    rows, mine = w_ref.shape[0], q_ref.shape[0]
    tensors = ((q_ref, hq_ref), (k_ref, hk_ref), (v_ref, hv_ref))
    greet(dp, seq, ndp, nseq)

    def row_half(ref, half):
        return ref.at[pl.ds(half * (rows // 2), rows // 2), :]

    ring = Ring(row_half, w_buf, dp, seq, ndp, w_send, w_recv, f_send, f_recv)

    def sides(step):
        other = lax.rem(dp + step, ndp)
        return pltpu.make_async_remote_copy(m_buf.at[:, columns(other, rows)], mc_ref.at[dp], m_send.at[step], m_recv.at[step],
                                            device_id=(other, seq), device_id_type=MESH)

    def spread(which, step):
        src, dst = tensors[which]
        other = lax.rem(seq + step, nseq)
        return pltpu.make_async_remote_copy(src.at[:, columns(other, HD)], dst.at[columns(seq, mine), :],
                                            a_send.at[which, step], a_recv.at[which, step], device_id=(dp, other), device_id_type=MESH)

    def keep(which):
        src, dst = tensors[which]
        return pltpu.make_async_copy(src.at[:, columns(seq, HD)], dst.at[columns(seq, mine), :], local.at[which])

    own_w = pltpu.make_async_copy(w_ref, w_buf.at[dp], local.at[3])
    own_m = pltpu.make_async_copy(m_ref, m_buf, local.at[4])
    own_c = pltpu.make_async_copy(m_buf.at[:, columns(dp, rows)], mc_ref.at[dp], local.at[5])
    own_w.start()
    own_m.start()
    ring.start(0, w_ref)
    ring.start(1, w_ref)
    for which in range(3):
        @pl.loop(1, nseq)
        def _(step):
            spread(which, step).start()
        keep(which).start()
    own_m.wait()
    for first in range(0, mine, HD):
        seen = jnp.broadcast_to(mask_ref[:, first:first + HD].astype(jnp.float32), (HD, HD)).T.astype(BF)
        for left in range(0, m_buf.shape[1], HD):
            m_buf[first:first + HD, left:left + HD] *= seen
    own_c.start()

    def late():
        @pl.loop(1, ndp)
        def _(step):
            sides(step).start()

    def store(slot):
        return pltpu.make_async_copy(w_buf.at[slot], wf_ref.at[slot], keep_w.at[slot])

    def give(head, source):
        return pltpu.make_async_remote_copy(g_buf.at[:, columns(head, HD)], hd_ref.at[columns(source, mine), :],
                                            a_send.at[3, head], a_recv.at[3, source], device_id=(dp, head), device_id_type=MESH)

    def own_g():
        return pltpu.make_async_copy(g_buf.at[:, columns(seq, HD)], hd_ref.at[columns(seq, mine), :], local.at[6])

    def use(slot):
        store(slot).start()
        g_buf[:, columns(slot, rows)] = lax.dot_general(m_buf[...], w_buf[slot], NT, preferred_element_type=jnp.float32).astype(BF)
        for half in range(rows // HD):
            head = slot * (rows // HD) + half

            @pl.when(head != seq)
            def _():
                give(head, seq).start()

            @pl.when(head == seq)
            def _():
                own_g().start()

    own_w.wait()
    ring.run(use, late)
    own_c.wait()

    @pl.loop(1, ndp)
    def _(step):
        sides(step).wait()

    @pl.loop(0, ndp)
    def _(slot):
        store(slot).wait()

    for which in range(3):
        @pl.loop(1, nseq)
        def _(step):
            spread(which, step).wait()
        keep(which).wait()

    own_g().wait()

    @pl.loop(0, nseq)
    def _(other):
        @pl.when(other != seq)
        def _():
            give(other, seq).wait_send()
            give(other, other).wait_recv()


def bring_in(mask, q, k, v, w, m):
    ndp, nseq = lax.axis_size("dp"), lax.axis_size("seq")
    mine, width = q.shape
    rows = w.shape[0]
    place = pl.BlockSpec(memory_space=pl.ANY)
    head = jax.ShapeDtypeStruct((mine * nseq, HD), BF)
    dma = pltpu.SemaphoreType.DMA
    return pl.pallas_call(
        bring,
        out_shape=(head,) * 4 + (jax.ShapeDtypeStruct((ndp, rows, width), BF), jax.ShapeDtypeStruct((ndp, mine, rows), BF)),
        in_specs=[pl.BlockSpec(memory_space=pltpu.VMEM)] + [place] * 5,
        out_specs=(place,) * 6,
        scratch_shapes=[
            pltpu.VMEM((ndp, rows, width), BF), pltpu.VMEM((mine, width), BF), pltpu.VMEM((mine, width), BF),
            dma((4, nseq)), dma((4, nseq)), dma((6,)), dma((6,)), dma((8,)), dma((8,)), dma((ndp,)), dma((ndp,)), dma((7,)), dma((ndp,))],
        compiler_params=pltpu.CompilerParams(collective_id=0, has_side_effects=True, vmem_limit_bytes=60 * 2**20),
        name="bring_in",
    )(mask, q, k, v, w, m)


def take(factor, o_ref, dq_ref, dk_ref, dv_ref, wf_ref, mc_ref, out_ref, oq_ref, ok_ref, ov_ref, wg_ref,
         a_buf, w_buf, c_buf, ct_buf, p_buf, part_buf, out_buf, wg_buf,
         o_send, o_recv, g_send, g_recv, r_send, r_recv, f_send, f_recv, p_send, p_recv, local):
    dp, seq = lax.axis_index("dp"), lax.axis_index("seq")
    ndp, nseq = lax.axis_size("dp"), lax.axis_size("seq")
    chips = ndp // 2
    z, core = dp // 2, lax.rem(dp, 2)
    mine, width = a_buf.shape[1:]
    rows = width // ndp
    tensors = ((dq_ref, oq_ref), (dk_ref, ok_ref), (dv_ref, ov_ref))
    greet(dp, seq, ndp, nseq)

    def slot(offset, other=False):
        return lax.rem(z + chips + offset, chips) * 2 + (1 - core if other else core)

    def head_at(step):
        return lax.rem(seq + nseq - step, nseq)

    def home(other, source):
        return pltpu.make_async_remote_copy(o_ref.at[columns(other, mine), :], a_buf.at[dp].at[:, columns(source, HD)],
                                            o_send.at[other], o_recv.at[source], device_id=(dp, other), device_id_type=MESH)

    def hop(kind, step):
        way = (1, -1, 1 - 2 * lax.rem(step, 2))[kind]
        origin = slot(0) if kind < 2 else slot(-way)
        piece = a_buf.at[origin].at[:, columns(head_at(step), HD)]
        return pltpu.make_async_remote_copy(piece, piece, r_send.at[kind, step], r_recv.at[kind, step],
                                            device_id=(slot(way), seq), device_id_type=MESH)

    def hand(kind, step):
        piece = a_buf.at[slot((0, -1, 1, 2)[kind])].at[:, columns(head_at(step), HD)]
        return pltpu.make_async_remote_copy(piece, piece, f_send.at[kind, step], f_recv.at[kind, step],
                                            device_id=(slot(0, True), seq), device_id_type=MESH)

    def spread(which, step):
        src, dst = tensors[which]
        other = lax.rem(seq + step, nseq)
        return pltpu.make_async_remote_copy(src.at[columns(other, mine), :], dst.at[:, columns(seq, HD)],
                                            g_send.at[which, step], g_recv.at[which, step], device_id=(dp, other), device_id_type=MESH)

    def keep(which):
        src, dst = tensors[which]
        return pltpu.make_async_copy(src.at[columns(seq, mine), :], dst.at[:, columns(seq, HD)], local.at[which])

    def share(head, source):
        return pltpu.make_async_remote_copy(p_buf.at[:, columns(head, HD)], part_buf.at[source],
                                            p_send.at[head], p_recv.at[source], device_id=(dp, head), device_id_type=MESH)

    own_p = pltpu.make_async_copy(p_buf.at[:, columns(seq, HD)], part_buf.at[seq], local.at[7])
    own_o = pltpu.make_async_copy(o_ref.at[columns(seq, mine), :], a_buf.at[dp].at[:, columns(seq, HD)], local.at[3])
    own_c = pltpu.make_async_copy(mc_ref, c_buf, local.at[4])
    own_w = pltpu.make_async_copy(wf_ref, w_buf, local.at[5])
    own_out = pltpu.make_async_copy(out_buf, out_ref, local.at[6])
    own_o.start()

    @pl.loop(1, nseq)
    def _(step):
        home(lax.rem(seq + step, nseq), seq).start()

    own_c.start()
    own_w.start()
    for which in range(3):
        @pl.loop(1, nseq)
        def _(step):
            spread(which, step).start()
        keep(which).start()

    own_c.wait()
    for source in range(ndp):
        ct_buf[:, source * mine:(source + 1) * mine] = c_buf[source].T
    own_o.wait()

    @pl.loop(0, nseq + 3)
    def _(turn):
        @pl.when(turn < nseq)
        def _():
            @pl.when(turn > 0)
            def _():
                home(head_at(turn), head_at(turn)).wait_recv()
            hop(0, turn).start()
            hop(1, turn).start()
            hand(0, turn).start()

        @pl.when((turn >= 1) & (turn < nseq + 1))
        def _():
            step = turn - 1
            hop(0, step).wait_recv()
            hop(1, step).wait_recv()
            hop(2, step).start()
            hand(1, step).start()
            hand(2, step).start()

        @pl.when((turn >= 2) & (turn < nseq + 2))
        def _():
            step = turn - 2
            hop(2, step).wait_recv()
            hand(3, step).start()

        @pl.when(turn >= 3)
        def _():
            step = turn - 3
            for kind in range(4):
                hand(kind, step).wait_recv()
            at = columns(head_at(step), HD)
            pieces = a_buf[:, :, at].reshape(ndp * mine, HD)
            p_buf[:, at] = jnp.dot(ct_buf[...], pieces, preferred_element_type=jnp.float32).astype(BF)

            @pl.when(step > 0)
            def _():
                share(head_at(step), seq).start()

            @pl.when(step == 0)
            def _():
                own_p.start()

    own_w.wait()

    @pl.loop(0, ndp)
    def _(tile):
        at = columns(tile, rows)
        total = jnp.zeros((mine, rows), jnp.float32)
        for source in range(ndp):
            total += jnp.dot(a_buf[dp, :, source * rows:(source + 1) * rows], w_buf[source, :, at], preferred_element_type=jnp.float32)
        out_buf[:, at] = total.astype(BF)

    own_out.start()
    own_p.wait()
    wg_buf[...] = part_buf[seq].astype(jnp.float32)

    @pl.loop(1, nseq)
    def _(step):
        source = lax.rem(seq + step, nseq)
        share(source, source).wait_recv()
        wg_buf[...] += part_buf[source].astype(jnp.float32)

    wg_ref[...] = wg_buf[...].T * factor
    for which in range(3):
        @pl.loop(1, nseq)
        def _(step):
            spread(which, step).wait()
        keep(which).wait()

    @pl.loop(0, nseq)
    def _(step):
        @pl.when(step > 0)
        def _():
            home(head_at(step), seq).wait_send()
            share(head_at(step), seq).wait_send()
        for kind in range(3):
            hop(kind, step).wait_send()
        for kind in range(4):
            hand(kind, step).wait_send()
    own_out.wait()


def take_home(o, dq, dk, dv, wf, mc):
    ndp, nseq = lax.axis_size("dp"), lax.axis_size("seq")
    mine, rows = mc.shape[1:]
    width = rows * ndp
    place = pl.BlockSpec(memory_space=pl.ANY)
    out = jax.ShapeDtypeStruct((mine, width), BF)
    dma = pltpu.SemaphoreType.DMA
    factor = 1.0 / math.sqrt(ndp * nseq * mine)
    return pl.pallas_call(
        functools.partial(take, factor),
        out_shape=(out,) * 4 + (jax.ShapeDtypeStruct((HD, rows), jnp.float32),),
        in_specs=[place] * 6,
        out_specs=(place,) * 4 + (pl.BlockSpec(memory_space=pltpu.VMEM),),
        scratch_shapes=[
            pltpu.VMEM((ndp, mine, width), BF), pltpu.VMEM((ndp, rows, width), BF), pltpu.VMEM((ndp, mine, rows), BF),
            pltpu.VMEM((rows, ndp * mine), BF), pltpu.VMEM((rows, width), BF),
            pltpu.VMEM((nseq, rows, HD), BF), pltpu.VMEM((mine, width), BF), pltpu.VMEM((rows, HD), jnp.float32),
            dma((nseq,)), dma((nseq,)), dma((3, nseq)), dma((3, nseq)), dma((3, nseq)), dma((3, nseq)), dma((4, nseq)), dma((4, nseq)),
            dma((nseq,)), dma((nseq,)), dma((8,))],
        compiler_params=pltpu.CompilerParams(collective_id=1, has_side_effects=True, vmem_limit_bytes=60 * 2**20),
        name="take_home",
    )(o, dq, dk, dv, wf, mc)

def attend(pat_ref, live_ref, q_ref, k_ref, v_ref, d_ref, o_ref, dq_ref, dk_ref, dv_ref, kt_ref, vt_ref, acc_ref, e_ref, g_ref, order_ref, fill_ref):
    nb = q_ref.shape[0] // BLOCK
    me = lax.axis_index("seq")
    levels = KMAX // STEP

    def block(index):
        return pl.ds(pl.multiple_of(index * BLOCK, BLOCK), BLOCK)

    def fold(x):
        return x.reshape(-1, 8, x.shape[-1])

    for level in range(levels):
        fill_ref[level] = 0
    @pl.loop(0, nb)
    def _(b):
        level = (live_ref[me, b] - 1) // STEP
        for later in range(1, levels):
            @pl.when(level < later)
            def _():
                fill_ref[later] += 1
    @pl.loop(0, nb)
    def _(b):
        level = (live_ref[me, b] - 1) // STEP
        order_ref[fill_ref[level]] = b
        fill_ref[level] += 1

    @pl.loop(0, nb // UNROLL)
    def _(turn):
        for i in range(UNROLL):
            rows = block(turn * UNROLL + i)
            kt_ref[rows, :] = k_ref[rows, :].T
            vt_ref[rows, :] = v_ref[rows, :].T
            acc_ref[rows, :] = jnp.zeros((BLOCK, 2 * HD), jnp.float32)

    none = jnp.zeros((BLOCK, HD), BF)

    def scores(count, b, at, base):
        live = live_ref[me, b]
        q = q_ref[block(b), :]
        d = d_ref[block(b), :]
        enter = jnp.concatenate([jnp.concatenate([q, none], 1), jnp.concatenate([none, d], 1)], 0)
        top = jnp.full((8, BLOCK), -1e30, jnp.float32)
        total = jnp.zeros((8, BLOCK), jnp.float32)
        mixed = jnp.zeros((8, BLOCK), jnp.float32)
        tops = []
        for j in range(0, count, GROUP):
            many = min(GROUP, count - j)
            both = lax.dot_general(
                jnp.concatenate([jnp.concatenate([k_ref[at[i], :], v_ref[at[i], :]], 1) for i in range(j, j + many)], 0),
                enter, NT, preferred_element_type=jnp.float32)
            s, g = both[:, :BLOCK], both[:, BLOCK:]
            if j + many > 1:
                parts = []
                for i in range(many):
                    part = s[i * BLOCK:(i + 1) * BLOCK]
                    parts.append(jnp.where(j + i < live, part, jnp.float32(-1e30)) if j + i > 0 else part)
                s = jnp.concatenate(parts, 0)
            new = jnp.maximum(top, jnp.max(fold(s), axis=0))
            old = jnp.exp((top - new) * SCALE)
            e = jnp.exp((fold(s) - new[None]) * SCALE)
            total = total * old + jnp.sum(e, axis=0)
            mixed = mixed * old + jnp.sum(e * fold(g), axis=0)
            e_ref[base + j * BLOCK:base + (j + many) * BLOCK, :] = e.reshape(many * BLOCK, BLOCK)
            g_ref[base + j * BLOCK:base + (j + many) * BLOCK, :] = g
            tops += [new] * many
            top = new
        peak = jnp.max(top, axis=0, keepdims=True)
        level = jnp.exp((top - peak) * SCALE)
        inverse = 1.0 / jnp.sum(total * level, axis=0, keepdims=True)
        delta = jnp.sum(mixed * level, axis=0, keepdims=True) * inverse
        return tops, peak, inverse, delta

    def grads(count, b, at, base, tops, peak, inverse, delta):
        q = q_ref[block(b), :]
        d = d_ref[block(b), :]
        leave = jnp.concatenate([jnp.concatenate([d, none], 1), jnp.concatenate([none, q], 1)], 0)
        o_sum = jnp.zeros((HD, BLOCK), jnp.float32)
        q_sum = jnp.zeros((HD, BLOCK), jnp.float32)
        for j in range(0, count, GROUP):
            many = min(GROUP, count - j)
            probs, slopes = [], []
            for i in range(j, j + many):
                e = e_ref[base + i * BLOCK:base + (i + 1) * BLOCK, :]
                g = g_ref[base + i * BLOCK:base + (i + 1) * BLOCK, :]
                weight = jnp.exp((tops[i] - peak) * SCALE) * inverse
                p = (fold(e) * weight[None]).reshape(BLOCK, BLOCK)
                probs.append(p.astype(BF))
                slopes.append((p * (g - delta)).astype(BF))
            pb, sb = jnp.concatenate(probs, 0), jnp.concatenate(slopes, 0)
            ps = jnp.concatenate([pb, sb], 1)
            out = jnp.dot(ps, leave, preferred_element_type=jnp.float32)
            for i in range(many):
                acc_ref[at[j + i], :] += out[i * BLOCK:(i + 1) * BLOCK]
            vt = jnp.concatenate([vt_ref[at[i], :] for i in range(j, j + many)], 1)
            kt = jnp.concatenate([kt_ref[at[i], :] for i in range(j, j + many)], 1)
            two = jnp.dot(jnp.concatenate([vt, kt], 0), ps, preferred_element_type=jnp.float32)
            o_sum += two[:HD, :BLOCK]
            q_sum += two[HD:, BLOCK:]
        o_ref[block(b), :] = o_sum.T.astype(BF)
        dq_ref[block(b), :] = (q_sum.T * SCALE).astype(BF)

    def with_slots(count, turn):
        bs = [order_ref[turn * PAIR + i] for i in range(PAIR)]
        ats = [[block(pat_ref[b, j]) for j in range(count)] for b in bs]
        states = [scores(count, b, at, i * KMAX * BLOCK) for i, (b, at) in enumerate(zip(bs, ats))]
        for i, (b, at, state) in enumerate(zip(bs, ats, states)):
            grads(count, b, at, i * KMAX * BLOCK, *state)

    @pl.loop(0, nb // PAIR)
    def _(turn):
        branches = [functools.partial(with_slots, c) for c in range(STEP, KMAX + 1, STEP)]
        longest = live_ref[me, order_ref[turn * PAIR + PAIR - 1]]
        lax.switch((longest - 1) // STEP, branches, turn)

    @pl.loop(0, nb // UNROLL)
    def _(turn):
        for i in range(UNROLL):
            rows = block(turn * UNROLL + i)
            dv_ref[rows, :] = acc_ref[rows, :HD].astype(BF)
            dk_ref[rows, :] = (acc_ref[rows, HD:] * SCALE).astype(BF)


def attention(q, k, v, d, pat, live):
    length = q.shape[0]
    out = jax.ShapeDtypeStruct((length, HD), BF)
    vm = pl.BlockSpec(memory_space=pltpu.VMEM)
    sm = pl.BlockSpec(memory_space=pltpu.SMEM)
    return pl.pallas_call(
        attend,
        out_shape=(out,) * 4,
        in_specs=[sm, sm, vm, vm, vm, vm],
        out_specs=(vm,) * 4,
        scratch_shapes=[
            pltpu.VMEM((length, HD), BF), pltpu.VMEM((length, HD), BF),
            pltpu.VMEM((length, 2 * HD), jnp.float32),
            pltpu.VMEM((PAIR * KMAX * BLOCK, BLOCK), jnp.float32), pltpu.VMEM((PAIR * KMAX * BLOCK, BLOCK), jnp.float32),
            pltpu.SMEM((length // BLOCK,), jnp.int32), pltpu.SMEM((KMAX // STEP,), jnp.int32)],
        compiler_params=pltpu.CompilerParams(vmem_limit_bytes=60 * 2**20),
        name="attention",
    )(pat, live, q, k, v, d)


def pass_on(*refs):
    arrays, sems = refs[:-1], refs[-1]
    count = len(arrays) // 2
    copies = [pltpu.make_async_copy(arrays[i], arrays[count + i], sems.at[i]) for i in range(count)]
    for copy in copies:
        copy.start()
    for copy in copies:
        copy.wait()


def hand_over(*arrays):
    place = pl.BlockSpec(memory_space=pl.ANY)
    return pl.pallas_call(
        pass_on,
        out_shape=tuple(jax.ShapeDtypeStruct(x.shape, x.dtype) for x in arrays),
        in_specs=[place] * len(arrays),
        out_specs=(place,) * len(arrays),
        scratch_shapes=[pltpu.SemaphoreType.DMA((len(arrays),))],
        compiler_params=pltpu.CompilerParams(vmem_limit_bytes=60 * 2**20),
        name="hand_over",
    )(*arrays)


def local(queries, keys, values, weight_out, cotangent, hidden_mask, pattern, live_slots):
    seq = lax.axis_index("seq")
    pat = lax.dynamic_index_in_dim(pattern, seq, 0, keepdims=False)
    q, k, v, d, weights, sides = bring_in(hidden_mask, queries[0], keys[0], values[0], weight_out, cotangent[0])
    attn, dq, dk, dv = attention(q, k, v, d, pat, live_slots)
    block_out, dq, dk, dv, weight_grad = hand_over(*take_home(attn, dq, dk, dv, weights, sides))
    return (block_out[None], dq[None], dk[None], dv[None], weight_grad)


def solution(mesh):
    rows = P("dp", "seq", None)
    return jax.shard_map(
        local,
        mesh=mesh,
        in_specs=(rows, rows, rows, P("dp", None), rows, P("dp", "seq"), P(), P()),
        out_specs=(rows, rows, rows, rows, P("seq", "dp")),
        check_vma=False,
    )
```

```python
import functools
import math

import jax
import jax.numpy as jnp
from jax import lax
from jax.experimental import pallas as pl
from jax.experimental.pallas import tpu as pltpu
from jax.sharding import PartitionSpec as P

HD = 128
BLOCK = 128
SIDE = 4
KMAX = 16
STEP = 2
GROUP = 2
PAIR = 4
UNROLL = 4
SCALE = 1.0 / math.sqrt(HD)
BF = jnp.bfloat16
MESH = pl.DeviceIdType.MESH
NT = (((1,), (1,)), ((), ()))
SHIFTS = ((1, 0), (0, 1), (3, 0), (0, 3), (1, 1), (3, 3), (1, 3), (3, 1), (2, 1), (1, 2), (2, 3), (3, 2), (2, 0), (0, 2), (2, 2))


def shifted(seq, step, back=False):
    dx, dy = SHIFTS[step]
    sign = -1 if back else 1
    return lax.rem(seq // SIDE + SIDE + sign * dx, SIDE) * SIDE + lax.rem(lax.rem(seq, SIDE) + SIDE + sign * dy, SIDE)


def columns(index, width):
    return pl.ds(pl.multiple_of(index * width, width), width)


def greet(dp, seq, ndp, nseq):
    barrier = pltpu.get_barrier_semaphore()

    @pl.loop(1, nseq)
    def _(step):
        pl.semaphore_signal(barrier, inc=1, device_id=(dp, lax.rem(seq + step, nseq)), device_id_type=MESH)

    @pl.loop(1, ndp)
    def _(step):
        pl.semaphore_signal(barrier, inc=1, device_id=(lax.rem(dp + step, ndp), seq), device_id_type=MESH)

    pl.semaphore_wait(barrier, nseq + ndp - 2)


class Ring:
    def __init__(self, part, buf, dp, seq, ndp, send, recv, give, take):
        self.part, self.buf, self.dp, self.seq = part, buf, dp, seq
        self.chips = ndp // 2
        self.z, self.core = dp // 2, lax.rem(dp, 2)
        self.send, self.recv, self.give, self.take = send, recv, give, take

    def slot(self, offset, other=False):
        core = 1 - self.core if other else self.core
        return lax.rem(self.z + self.chips + offset, self.chips) * 2 + core

    def half(self, slot, half):
        return self.part(self.buf.at[slot], half)

    def hop(self, index, source=None):
        up = index % 2 == 0
        half = (0, 1, 1, 0, 0, 1)[index]
        slot = self.slot(0) if index < 4 else self.slot(-1 if up else 1)
        target = self.slot(1 if up else -1)
        src = self.half(slot, half) if source is None else self.part(source, half)
        return pltpu.make_async_remote_copy(src, self.half(slot, half), self.send.at[index], self.recv.at[index],
                                            device_id=(target, self.seq), device_id_type=MESH)

    def hand(self, index, source=None):
        if index < 2:
            slot, half = self.slot(0), index
        else:
            slot = self.slot((-1, 1, -1, 1, 2, 2)[index - 2])
            half = (0, 1, 1, 0, 0, 1)[index - 2]
        src = self.half(slot, half) if source is None else self.part(source, half)
        return pltpu.make_async_remote_copy(src, self.half(slot, half), self.give.at[index], self.take.at[index],
                                            device_id=(self.slot(0, True), self.seq), device_id_type=MESH)

    def start(self, half, source=None):
        for index in ((0, 3), (1, 2))[half]:
            self.hop(index, source).start()
        self.hand(half, source).start()

    def run(self, use, late):
        use(self.slot(0))
        for index in (0, 1):
            self.hop(index).wait_recv()
            self.hop(index + 4).start()
            self.hand(index + 2).start()
        self.hand(0).wait_recv()
        self.hand(1).wait_recv()
        use(self.slot(0, True))
        for index, offset in ((2, -1), (3, 1)):
            self.hop(index).wait_recv()
            self.hand(index + 2).start()
            use(self.slot(offset))
        for first, second, offset in ((2, 4, -1), (3, 5, 1)):
            self.hand(first).wait_recv()
            self.hand(second).wait_recv()
            use(self.slot(offset, True))
        for index in (4, 5):
            self.hop(index).wait_recv()
            self.hand(index + 2).start()
        late()
        use(self.slot(2))
        self.hand(6).wait_recv()
        self.hand(7).wait_recv()
        use(self.slot(2, True))
        for index in range(6):
            self.hop(index).wait_send()
        for index in range(8):
            self.hand(index).wait_send()


def bring(mask_ref, q_ref, k_ref, v_ref, w_ref, m_ref, hq_ref, hk_ref, hv_ref, hd_ref, wf_ref, mc_ref,
          w_buf, m_buf, g_buf, a_send, a_recv, w_send, w_recv, f_send, f_recv, m_send, m_recv, local, keep_w):
    dp, seq = lax.axis_index("dp"), lax.axis_index("seq")
    ndp, nseq = lax.axis_size("dp"), lax.axis_size("seq")
    rows, mine = w_ref.shape[0], q_ref.shape[0]
    tensors = ((q_ref, hq_ref), (k_ref, hk_ref), (v_ref, hv_ref))
    greet(dp, seq, ndp, nseq)

    def row_half(ref, half):
        return ref.at[pl.ds(half * (rows // 2), rows // 2), :]

    ring = Ring(row_half, w_buf, dp, seq, ndp, w_send, w_recv, f_send, f_recv)

    def sides(step):
        other = lax.rem(dp + step, ndp)
        return pltpu.make_async_remote_copy(m_buf.at[:, columns(other, rows)], mc_ref.at[dp], m_send.at[step], m_recv.at[step],
                                            device_id=(other, seq), device_id_type=MESH)

    def spread(which, step):
        src, dst = tensors[which]
        other = shifted(seq, step)
        return pltpu.make_async_remote_copy(src.at[:, columns(other, HD)], dst.at[columns(seq, mine), :],
                                            a_send.at[which, step], a_recv.at[which, step], device_id=(dp, other), device_id_type=MESH)

    def keep(which):
        src, dst = tensors[which]
        return pltpu.make_async_copy(src.at[:, columns(seq, HD)], dst.at[columns(seq, mine), :], local.at[which])

    own_w = pltpu.make_async_copy(w_ref, w_buf.at[dp], local.at[3])
    own_m = pltpu.make_async_copy(m_ref, m_buf, local.at[4])
    own_c = pltpu.make_async_copy(m_buf.at[:, columns(dp, rows)], mc_ref.at[dp], local.at[5])
    own_w.start()
    own_m.start()
    ring.start(0, w_ref)
    ring.start(1, w_ref)
    for which in range(3):
        for step in range(nseq - 1):
            spread(which, step).start()
        keep(which).start()
    own_m.wait()
    for first in range(0, mine, HD):
        seen = jnp.broadcast_to(mask_ref[:, first:first + HD].astype(jnp.float32), (HD, HD)).T.astype(BF)
        for left in range(0, m_buf.shape[1], HD):
            m_buf[first:first + HD, left:left + HD] *= seen
    own_c.start()

    def late():
        @pl.loop(1, ndp)
        def _(step):
            sides(step).start()

    def store(slot):
        return pltpu.make_async_copy(w_buf.at[slot], wf_ref.at[slot], keep_w.at[slot])

    def give(head, source):
        return pltpu.make_async_remote_copy(g_buf.at[:, columns(head, HD)], hd_ref.at[columns(source, mine), :],
                                            a_send.at[3, head], a_recv.at[3, source], device_id=(dp, head), device_id_type=MESH)

    def own_g():
        return pltpu.make_async_copy(g_buf.at[:, columns(seq, HD)], hd_ref.at[columns(seq, mine), :], local.at[6])

    def use(slot):
        store(slot).start()
        g_buf[:, columns(slot, rows)] = lax.dot_general(m_buf[...], w_buf[slot], NT, preferred_element_type=jnp.float32).astype(BF)
        for half in range(rows // HD):
            head = slot * (rows // HD) + half

            @pl.when(head != seq)
            def _():
                give(head, seq).start()

            @pl.when(head == seq)
            def _():
                own_g().start()

    own_w.wait()
    ring.run(use, late)
    own_c.wait()

    @pl.loop(1, ndp)
    def _(step):
        sides(step).wait()

    @pl.loop(0, ndp)
    def _(slot):
        store(slot).wait()

    for which in range(3):
        for step in range(nseq - 1):
            spread(which, step).wait()
        keep(which).wait()

    own_g().wait()

    @pl.loop(0, nseq)
    def _(other):
        @pl.when(other != seq)
        def _():
            give(other, seq).wait_send()
            give(other, other).wait_recv()


def bring_in(mask, q, k, v, w, m):
    ndp, nseq = lax.axis_size("dp"), lax.axis_size("seq")
    mine, width = q.shape
    rows = w.shape[0]
    place = pl.BlockSpec(memory_space=pl.ANY)
    head = jax.ShapeDtypeStruct((mine * nseq, HD), BF)
    dma = pltpu.SemaphoreType.DMA
    return pl.pallas_call(
        bring,
        out_shape=(head,) * 4 + (jax.ShapeDtypeStruct((ndp, rows, width), BF), jax.ShapeDtypeStruct((ndp, mine, rows), BF)),
        in_specs=[pl.BlockSpec(memory_space=pltpu.VMEM)] + [place] * 5,
        out_specs=(place,) * 6,
        scratch_shapes=[
            pltpu.VMEM((ndp, rows, width), BF), pltpu.VMEM((mine, width), BF), pltpu.VMEM((mine, width), BF),
            dma((4, nseq)), dma((4, nseq)), dma((6,)), dma((6,)), dma((8,)), dma((8,)), dma((ndp,)), dma((ndp,)), dma((7,)), dma((ndp,))],
        compiler_params=pltpu.CompilerParams(collective_id=0, has_side_effects=True, vmem_limit_bytes=60 * 2**20),
        name="bring_in",
    )(mask, q, k, v, w, m)


def take(factor, o_ref, dq_ref, dk_ref, dv_ref, wf_ref, mc_ref, out_ref, oq_ref, ok_ref, ov_ref, wg_ref,
         a_buf, w_buf, c_buf, ct_buf, p_buf, part_buf, out_buf, wg_buf,
         o_send, o_recv, g_send, g_recv, r_send, r_recv, f_send, f_recv, p_send, p_recv, local):
    dp, seq = lax.axis_index("dp"), lax.axis_index("seq")
    ndp, nseq = lax.axis_size("dp"), lax.axis_size("seq")
    chips = ndp // 2
    z, core = dp // 2, lax.rem(dp, 2)
    mine, width = a_buf.shape[1:]
    rows = width // ndp
    turns = nseq // 2
    wide = 2 * HD
    tensors = ((dq_ref, oq_ref), (dk_ref, ok_ref), (dv_ref, ov_ref))
    greet(dp, seq, ndp, nseq)

    def slot(offset, other=False):
        return lax.rem(z + chips + offset, chips) * 2 + (1 - core if other else core)

    def pair_at(step):
        return lax.rem(seq // SIDE + SIDE - lax.rem(step, SIDE), SIDE) * 2 + lax.rem(lax.rem(seq, SIDE) // 2 + step // SIDE, 2)

    def target(step):
        turn = step // 2
        return (lax.rem(seq // SIDE + lax.rem(turn, SIDE), SIDE) * 2 + lax.rem(lax.rem(seq, SIDE) // 2 + turn // SIDE, 2)) * 2 + lax.rem(step, 2)

    def home(other, source):
        return pltpu.make_async_remote_copy(o_ref.at[columns(other, mine), :], a_buf.at[dp].at[:, columns(source, HD)],
                                            o_send.at[other], o_recv.at[source], device_id=(dp, other), device_id_type=MESH)

    def hop(kind, step):
        way = (1, -1, 1 - 2 * lax.rem(step, 2))[kind]
        origin = slot(0) if kind < 2 else slot(-way)
        piece = a_buf.at[origin].at[:, columns(pair_at(step), wide)]
        return pltpu.make_async_remote_copy(piece, piece, r_send.at[kind, step], r_recv.at[kind, step],
                                            device_id=(slot(way), seq), device_id_type=MESH)

    def hand(kind, step):
        piece = a_buf.at[slot((0, -1, 1, 2)[kind])].at[:, columns(pair_at(step), wide)]
        return pltpu.make_async_remote_copy(piece, piece, f_send.at[kind, step], f_recv.at[kind, step],
                                            device_id=(slot(0, True), seq), device_id_type=MESH)

    def spread(which, step):
        src, dst = tensors[which]
        other = shifted(seq, step)
        return pltpu.make_async_remote_copy(src.at[columns(other, mine), :], dst.at[:, columns(seq, HD)],
                                            g_send.at[which, step], g_recv.at[which, step], device_id=(dp, other), device_id_type=MESH)

    def keep(which):
        src, dst = tensors[which]
        return pltpu.make_async_copy(src.at[columns(seq, mine), :], dst.at[:, columns(seq, HD)], local.at[which])

    def share(head, source):
        return pltpu.make_async_remote_copy(p_buf.at[:, columns(head, HD)], part_buf.at[source],
                                            p_send.at[head], p_recv.at[source], device_id=(dp, head), device_id_type=MESH)

    own_p = pltpu.make_async_copy(p_buf.at[:, columns(seq, HD)], part_buf.at[seq], local.at[7])
    own_o = pltpu.make_async_copy(o_ref.at[columns(seq, mine), :], a_buf.at[dp].at[:, columns(seq, HD)], local.at[3])
    own_c = pltpu.make_async_copy(mc_ref, c_buf, local.at[4])
    own_w = pltpu.make_async_copy(wf_ref, w_buf, local.at[5])
    own_out = pltpu.make_async_copy(out_buf, out_ref, local.at[6])
    own_o.start()

    @pl.loop(0, nseq)
    def _(step):
        @pl.when(target(step) != seq)
        def _():
            home(target(step), seq).start()

    own_c.start()
    own_w.start()
    for which in range(3):
        for step in range(nseq - 1):
            spread(which, step).start()
        keep(which).start()

    own_c.wait()
    for source in range(ndp):
        ct_buf[:, source * mine:(source + 1) * mine] = c_buf[source].T
    own_o.wait()

    def project(tile):
        at = columns(tile, rows)
        total = jnp.zeros((mine, rows), jnp.float32)
        for source in range(ndp):
            total += jnp.dot(a_buf[dp, :, source * rows:(source + 1) * rows], w_buf[source, :, at], preferred_element_type=jnp.float32)
        out_buf[:, at] = total.astype(BF)

    @pl.loop(0, turns + 3)
    def _(turn):
        @pl.when(turn < turns)
        def _():
            for side in range(2):
                head = pair_at(turn) * 2 + side

                @pl.when(head != seq)
                def _():
                    home(head, head).wait_recv()
            hop(0, turn).start()
            hop(1, turn).start()
            hand(0, turn).start()

        @pl.when((turn >= 1) & (turn < turns + 1))
        def _():
            step = turn - 1
            hop(0, step).wait_recv()
            hop(1, step).wait_recv()
            hop(2, step).start()
            hand(1, step).start()
            hand(2, step).start()

        @pl.when((turn >= 2) & (turn < turns + 2))
        def _():
            step = turn - 2
            hop(2, step).wait_recv()
            hand(3, step).start()

        @pl.when(turn == turns - 1)
        def _():
            own_w.wait()

        @pl.when((turn >= turns - 1) & (turn < turns + 1))
        def _():
            @pl.loop(0, ndp // 2)
            def _(tile):
                project((turn - turns + 1) * (ndp // 2) + tile)

        @pl.when(turn >= 3)
        def _():
            step = turn - 3
            for kind in range(4):
                hand(kind, step).wait_recv()
            at = columns(pair_at(step), wide)
            pieces = a_buf[:, :, at].reshape(ndp * mine, wide)
            p_buf[:, at] = jnp.dot(ct_buf[...], pieces, preferred_element_type=jnp.float32).astype(BF)
            for side in range(2):
                head = pair_at(step) * 2 + side

                @pl.when(head != seq)
                def _():
                    share(head, seq).start()

                @pl.when(head == seq)
                def _():
                    own_p.start()

    own_out.start()
    own_p.wait()
    wg_buf[...] = part_buf[seq].astype(jnp.float32)

    @pl.loop(1, nseq)
    def _(step):
        source = lax.rem(seq + step, nseq)
        share(source, source).wait_recv()
        wg_buf[...] += part_buf[source].astype(jnp.float32)

    wg_ref[...] = wg_buf[...].T * factor
    for which in range(3):
        for step in range(nseq - 1):
            spread(which, step).wait()
        keep(which).wait()

    @pl.loop(1, nseq)
    def _(step):
        home(lax.rem(seq + step, nseq), seq).wait_send()
        share(lax.rem(seq + step, nseq), seq).wait_send()

    @pl.loop(0, turns)
    def _(step):
        for kind in range(3):
            hop(kind, step).wait_send()
        for kind in range(4):
            hand(kind, step).wait_send()
    own_out.wait()


def take_home(o, dq, dk, dv, wf, mc):
    ndp, nseq = lax.axis_size("dp"), lax.axis_size("seq")
    mine, rows = mc.shape[1:]
    width = rows * ndp
    place = pl.BlockSpec(memory_space=pl.ANY)
    out = jax.ShapeDtypeStruct((mine, width), BF)
    dma = pltpu.SemaphoreType.DMA
    factor = 1.0 / math.sqrt(ndp * nseq * mine)
    return pl.pallas_call(
        functools.partial(take, factor),
        out_shape=(out,) * 4 + (jax.ShapeDtypeStruct((HD, rows), jnp.float32),),
        in_specs=[place] * 6,
        out_specs=(place,) * 4 + (pl.BlockSpec(memory_space=pltpu.VMEM),),
        scratch_shapes=[
            pltpu.VMEM((ndp, mine, width), BF), pltpu.VMEM((ndp, rows, width), BF), pltpu.VMEM((ndp, mine, rows), BF),
            pltpu.VMEM((rows, ndp * mine), BF), pltpu.VMEM((rows, width), BF),
            pltpu.VMEM((nseq, rows, HD), BF), pltpu.VMEM((mine, width), BF), pltpu.VMEM((rows, HD), jnp.float32),
            dma((nseq,)), dma((nseq,)), dma((3, nseq)), dma((3, nseq)), dma((3, nseq // 2)), dma((3, nseq // 2)), dma((4, nseq // 2)), dma((4, nseq // 2)),
            dma((nseq,)), dma((nseq,)), dma((8,))],
        compiler_params=pltpu.CompilerParams(collective_id=1, has_side_effects=True, vmem_limit_bytes=60 * 2**20),
        name="take_home",
    )(o, dq, dk, dv, wf, mc)

def attend(pat_ref, live_ref, q_ref, k_ref, v_ref, d_ref, o_ref, dq_ref, dk_ref, dv_ref, kt_ref, vt_ref, acc_ref, e_ref, g_ref, order_ref, fill_ref):
    nb = q_ref.shape[0] // BLOCK
    me = lax.axis_index("seq")
    levels = KMAX // STEP

    def block(index):
        return pl.ds(pl.multiple_of(index * BLOCK, BLOCK), BLOCK)

    def fold(x):
        return x.reshape(-1, 8, x.shape[-1])

    for level in range(levels):
        fill_ref[level] = 0
    @pl.loop(0, nb)
    def _(b):
        level = (live_ref[me, b] - 1) // STEP
        for later in range(1, levels):
            @pl.when(level < later)
            def _():
                fill_ref[later] += 1
    @pl.loop(0, nb)
    def _(b):
        level = (live_ref[me, b] - 1) // STEP
        order_ref[fill_ref[level]] = b
        fill_ref[level] += 1

    @pl.loop(0, nb // UNROLL)
    def _(turn):
        for i in range(UNROLL):
            rows = block(turn * UNROLL + i)
            kt_ref[rows, :] = k_ref[rows, :].T
            vt_ref[rows, :] = v_ref[rows, :].T
            acc_ref[rows, :] = jnp.zeros((BLOCK, 2 * HD), jnp.float32)

    none = jnp.zeros((BLOCK, HD), BF)

    def scores(count, b, at, base):
        live = live_ref[me, b]
        q = q_ref[block(b), :]
        d = d_ref[block(b), :]
        enter = jnp.concatenate([jnp.concatenate([q, none], 1), jnp.concatenate([none, d], 1)], 0)
        top = jnp.full((8, BLOCK), -1e30, jnp.float32)
        total = jnp.zeros((8, BLOCK), jnp.float32)
        mixed = jnp.zeros((8, BLOCK), jnp.float32)
        tops = []
        for j in range(0, count, GROUP):
            many = min(GROUP, count - j)
            both = lax.dot_general(
                jnp.concatenate([jnp.concatenate([k_ref[at[i], :], v_ref[at[i], :]], 1) for i in range(j, j + many)], 0),
                enter, NT, preferred_element_type=jnp.float32)
            s, g = both[:, :BLOCK], both[:, BLOCK:]
            if j + many > 1:
                parts = []
                for i in range(many):
                    part = s[i * BLOCK:(i + 1) * BLOCK]
                    parts.append(jnp.where(j + i < live, part, jnp.float32(-1e30)) if j + i > 0 else part)
                s = jnp.concatenate(parts, 0)
            new = jnp.maximum(top, jnp.max(fold(s), axis=0))
            old = jnp.exp((top - new) * SCALE)
            e = jnp.exp((fold(s) - new[None]) * SCALE)
            total = total * old + jnp.sum(e, axis=0)
            mixed = mixed * old + jnp.sum(e * fold(g), axis=0)
            e_ref[base + j * BLOCK:base + (j + many) * BLOCK, :] = e.reshape(many * BLOCK, BLOCK)
            g_ref[base + j * BLOCK:base + (j + many) * BLOCK, :] = g
            tops += [new] * many
            top = new
        peak = jnp.max(top, axis=0, keepdims=True)
        level = jnp.exp((top - peak) * SCALE)
        inverse = 1.0 / jnp.sum(total * level, axis=0, keepdims=True)
        delta = jnp.sum(mixed * level, axis=0, keepdims=True) * inverse
        return tops, peak, inverse, delta

    def grads(count, b, at, base, tops, peak, inverse, delta):
        q = q_ref[block(b), :]
        d = d_ref[block(b), :]
        leave = jnp.concatenate([jnp.concatenate([d, none], 1), jnp.concatenate([none, q], 1)], 0)
        o_sum = jnp.zeros((HD, BLOCK), jnp.float32)
        q_sum = jnp.zeros((HD, BLOCK), jnp.float32)
        for j in range(0, count, GROUP):
            many = min(GROUP, count - j)
            probs, slopes = [], []
            for i in range(j, j + many):
                e = e_ref[base + i * BLOCK:base + (i + 1) * BLOCK, :]
                g = g_ref[base + i * BLOCK:base + (i + 1) * BLOCK, :]
                weight = jnp.exp((tops[i] - peak) * SCALE) * inverse
                p = (fold(e) * weight[None]).reshape(BLOCK, BLOCK)
                probs.append(p.astype(BF))
                slopes.append((p * (g - delta)).astype(BF))
            pb, sb = jnp.concatenate(probs, 0), jnp.concatenate(slopes, 0)
            ps = jnp.concatenate([pb, sb], 1)
            out = jnp.dot(ps, leave, preferred_element_type=jnp.float32)
            for i in range(many):
                acc_ref[at[j + i], :] += out[i * BLOCK:(i + 1) * BLOCK]
            vt = jnp.concatenate([vt_ref[at[i], :] for i in range(j, j + many)], 1)
            kt = jnp.concatenate([kt_ref[at[i], :] for i in range(j, j + many)], 1)
            two = jnp.dot(jnp.concatenate([vt, kt], 0), ps, preferred_element_type=jnp.float32)
            o_sum += two[:HD, :BLOCK]
            q_sum += two[HD:, BLOCK:]
        o_ref[block(b), :] = o_sum.T.astype(BF)
        dq_ref[block(b), :] = (q_sum.T * SCALE).astype(BF)

    def with_slots(count, turn):
        bs = [order_ref[turn * PAIR + i] for i in range(PAIR)]
        ats = [[block(pat_ref[b, j]) for j in range(count)] for b in bs]
        states = [scores(count, b, at, i * KMAX * BLOCK) for i, (b, at) in enumerate(zip(bs, ats))]
        for i, (b, at, state) in enumerate(zip(bs, ats, states)):
            grads(count, b, at, i * KMAX * BLOCK, *state)

    @pl.loop(0, nb // PAIR)
    def _(turn):
        branches = [functools.partial(with_slots, c) for c in range(STEP, KMAX + 1, STEP)]
        longest = live_ref[me, order_ref[turn * PAIR + PAIR - 1]]
        lax.switch((longest - 1) // STEP, branches, turn)

    @pl.loop(0, nb // UNROLL)
    def _(turn):
        for i in range(UNROLL):
            rows = block(turn * UNROLL + i)
            dv_ref[rows, :] = acc_ref[rows, :HD].astype(BF)
            dk_ref[rows, :] = (acc_ref[rows, HD:] * SCALE).astype(BF)


def attention(q, k, v, d, pat, live):
    length = q.shape[0]
    out = jax.ShapeDtypeStruct((length, HD), BF)
    vm = pl.BlockSpec(memory_space=pltpu.VMEM)
    sm = pl.BlockSpec(memory_space=pltpu.SMEM)
    return pl.pallas_call(
        attend,
        out_shape=(out,) * 4,
        in_specs=[sm, sm, vm, vm, vm, vm],
        out_specs=(vm,) * 4,
        scratch_shapes=[
            pltpu.VMEM((length, HD), BF), pltpu.VMEM((length, HD), BF),
            pltpu.VMEM((length, 2 * HD), jnp.float32),
            pltpu.VMEM((PAIR * KMAX * BLOCK, BLOCK), jnp.float32), pltpu.VMEM((PAIR * KMAX * BLOCK, BLOCK), jnp.float32),
            pltpu.SMEM((length // BLOCK,), jnp.int32), pltpu.SMEM((KMAX // STEP,), jnp.int32)],
        compiler_params=pltpu.CompilerParams(vmem_limit_bytes=60 * 2**20),
        name="attention",
    )(pat, live, q, k, v, d)


def pass_on(*refs):
    count = (len(refs) - 1) // 3
    sources, results, stops, sems = refs[:count], refs[count:2 * count], refs[2 * count:3 * count], refs[-1]
    fetches = [pltpu.make_async_copy(sources[i], stops[i], sems.at[0, i]) for i in range(count)]
    stores = [pltpu.make_async_copy(stops[i], results[i], sems.at[1, i]) for i in range(count)]
    for fetch in fetches:
        fetch.start()
    for fetch, store in zip(fetches, stores):
        fetch.wait()
        store.start()
    for store in stores:
        store.wait()


def hand_over(*arrays):
    place = pl.BlockSpec(memory_space=pl.ANY)
    return pl.pallas_call(
        pass_on,
        out_shape=tuple(jax.ShapeDtypeStruct(x.shape, x.dtype) for x in arrays),
        in_specs=[place] * len(arrays),
        out_specs=(place,) * len(arrays),
        scratch_shapes=[pltpu.VMEM(x.shape, x.dtype) for x in arrays] + [pltpu.SemaphoreType.DMA((2, len(arrays)))],
        compiler_params=pltpu.CompilerParams(vmem_limit_bytes=60 * 2**20),
        name="hand_over",
    )(*arrays)


def local(queries, keys, values, weight_out, cotangent, hidden_mask, pattern, live_slots):
    seq = lax.axis_index("seq")
    pat = lax.dynamic_index_in_dim(pattern, seq, 0, keepdims=False)
    q, k, v, d, weights, sides = bring_in(hidden_mask, queries[0], keys[0], values[0], weight_out, cotangent[0])
    attn, dq, dk, dv = attention(q, k, v, d, pat, live_slots)
    block_out, dq, dk, dv, weight_grad = hand_over(*take_home(attn, dq, dk, dv, weights, sides))
    return (block_out[None], dq[None], dk[None], dv[None], weight_grad)


def solution(mesh):
    rows = P("dp", "seq", None)
    return jax.shard_map(
        local,
        mesh=mesh,
        in_specs=(rows, rows, rows, P("dp", None), rows, P("dp", "seq"), P(), P()),
        out_specs=(rows, rows, rows, rows, P("seq", "dp")),
        check_vma=False,
    )
```

```python
import functools
import math

import jax
import jax.numpy as jnp
from jax import lax
from jax.experimental import pallas as pl
from jax.experimental.pallas import tpu as pltpu
from jax.sharding import PartitionSpec as P

HD = 128
BLOCK = 128
SIDE = 4
PIECE = 32
KMAX = 16
STEP = 2
GROUP = 2
PAIR = 4
UNROLL = 4
SCALE = 1.0 / math.sqrt(HD)
BF = jnp.bfloat16
MESH = pl.DeviceIdType.MESH
NT = (((1,), (1,)), ((), ()))
SHIFTS = ((1, 0), (0, 1), (3, 0), (0, 3), (1, 1), (3, 3), (1, 3), (3, 1), (2, 1), (1, 2), (2, 3), (3, 2), (2, 0), (0, 2), (2, 2))


def shifted(seq, step, back=False):
    dx, dy = SHIFTS[step]
    sign = -1 if back else 1
    return lax.rem(seq // SIDE + SIDE + sign * dx, SIDE) * SIDE + lax.rem(lax.rem(seq, SIDE) + SIDE + sign * dy, SIDE)


def columns(index, width):
    return pl.ds(pl.multiple_of(index * width, width), width)


def greet(dp, seq, ndp, nseq):
    barrier = pltpu.get_barrier_semaphore()

    @pl.loop(1, nseq)
    def _(step):
        pl.semaphore_signal(barrier, inc=1, device_id=(dp, lax.rem(seq + step, nseq)), device_id_type=MESH)

    @pl.loop(1, ndp)
    def _(step):
        pl.semaphore_signal(barrier, inc=1, device_id=(lax.rem(dp + step, ndp), seq), device_id_type=MESH)

    pl.semaphore_wait(barrier, nseq + ndp - 2)


class Ring:
    def __init__(self, shard, buf, dp, seq, ndp, send, recv, give, take):
        self.shard, self.buf, self.dp, self.seq = shard, buf, dp, seq
        self.chips = ndp // 2
        self.pieces = shard.shape[0] // PIECE
        self.z, self.core = dp // 2, lax.rem(dp, 2)
        self.send, self.recv, self.give, self.take = send, recv, give, take

    def slot(self, offset, other=False):
        core = 1 - self.core if other else self.core
        return lax.rem(self.z + self.chips + offset, self.chips) * 2 + core

    def piece(self, ref, index):
        return ref.at[columns(index, PIECE), :]

    def hop(self, kind, index):
        way = (1, -1, 1 - 2 * lax.rem(index, 2))[kind]
        origin = self.slot(0) if kind < 2 else self.slot(-way)
        there = self.piece(self.buf.at[origin], index)
        return pltpu.make_async_remote_copy(self.piece(self.shard, index) if kind < 2 else there, there,
                                            self.send.at[kind, index], self.recv.at[kind, index],
                                            device_id=(self.slot(way), self.seq), device_id_type=MESH)

    def hand(self, kind, index):
        there = self.piece(self.buf.at[self.slot((0, -1, 1, 2)[kind])], index)
        return pltpu.make_async_remote_copy(self.piece(self.shard, index) if kind == 0 else there, there,
                                            self.give.at[kind, index], self.take.at[kind, index],
                                            device_id=(self.slot(0, True), self.seq), device_id_type=MESH)

    def start(self):
        @pl.loop(0, self.pieces)
        def _(index):
            self.hop(0, index).start()
            self.hop(1, index).start()

        @pl.loop(0, self.pieces)
        def _(index):
            self.hand(0, index).start()

    def taken(self, *kinds):
        @pl.loop(0, self.pieces)
        def _(index):
            for kind in kinds:
                self.hand(kind, index).wait_recv()

    def run(self, use, late):
        use(self.slot(0))
        self.taken(0)
        use(self.slot(0, True))

        @pl.loop(0, self.pieces)
        def _(index):
            self.hop(0, index).wait_recv()
            self.hop(1, index).wait_recv()
            self.hop(2, index).start()
            self.hand(1, index).start()
            self.hand(2, index).start()

        use(self.slot(-1))
        use(self.slot(1))
        self.taken(1, 2)
        use(self.slot(-1, True))
        use(self.slot(1, True))

        @pl.loop(0, self.pieces)
        def _(index):
            self.hop(2, index).wait_recv()
            self.hand(3, index).start()

        late()
        use(self.slot(2))
        self.taken(3)
        use(self.slot(2, True))

        @pl.loop(0, self.pieces)
        def _(index):
            for kind in range(3):
                self.hop(kind, index).wait_send()
            for kind in range(4):
                self.hand(kind, index).wait_send()


def bring(mask_ref, q_ref, k_ref, v_ref, w_ref, m_ref, hq_ref, hk_ref, hv_ref, hd_ref, wf_ref, mc_ref,
          w_buf, m_buf, g_buf, a_send, a_recv, w_send, w_recv, f_send, f_recv, m_send, m_recv, local, keep_w):
    dp, seq = lax.axis_index("dp"), lax.axis_index("seq")
    ndp, nseq = lax.axis_size("dp"), lax.axis_size("seq")
    rows, mine = w_ref.shape[0], q_ref.shape[0]
    tensors = ((q_ref, hq_ref), (k_ref, hk_ref), (v_ref, hv_ref))
    greet(dp, seq, ndp, nseq)

    ring = Ring(w_ref, w_buf, dp, seq, ndp, w_send, w_recv, f_send, f_recv)

    def sides(step):
        other = lax.rem(dp + step, ndp)
        return pltpu.make_async_remote_copy(m_buf.at[:, columns(other, rows)], mc_ref.at[dp], m_send.at[step], m_recv.at[step],
                                            device_id=(other, seq), device_id_type=MESH)

    def spread(which, step):
        src, dst = tensors[which]
        other = shifted(seq, step)
        return pltpu.make_async_remote_copy(src.at[:, columns(other, HD)], dst.at[columns(seq, mine), :],
                                            a_send.at[which, step], a_recv.at[which, step], device_id=(dp, other), device_id_type=MESH)

    def keep(which):
        src, dst = tensors[which]
        return pltpu.make_async_copy(src.at[:, columns(seq, HD)], dst.at[columns(seq, mine), :], local.at[which])

    own_w = pltpu.make_async_copy(w_ref, w_buf.at[dp], local.at[3])
    own_m = pltpu.make_async_copy(m_ref, m_buf, local.at[4])
    own_c = pltpu.make_async_copy(m_buf.at[:, columns(dp, rows)], mc_ref.at[dp], local.at[5])
    own_w.start()
    own_m.start()
    ring.start()
    for which in range(3):
        for step in range(nseq - 1):
            spread(which, step).start()
        keep(which).start()
    own_m.wait()
    for first in range(0, mine, HD):
        seen = jnp.broadcast_to(mask_ref[:, first:first + HD].astype(jnp.float32), (HD, HD)).T.astype(BF)
        for left in range(0, m_buf.shape[1], HD):
            m_buf[first:first + HD, left:left + HD] *= seen
    own_c.start()

    def late():
        @pl.loop(1, ndp)
        def _(step):
            sides(step).start()

    def store(slot):
        return pltpu.make_async_copy(w_buf.at[slot], wf_ref.at[slot], keep_w.at[slot])

    def give(head, source):
        return pltpu.make_async_remote_copy(g_buf.at[:, columns(head, HD)], hd_ref.at[columns(source, mine), :],
                                            a_send.at[3, head], a_recv.at[3, source], device_id=(dp, head), device_id_type=MESH)

    def own_g():
        return pltpu.make_async_copy(g_buf.at[:, columns(seq, HD)], hd_ref.at[columns(seq, mine), :], local.at[6])

    def use(slot):
        store(slot).start()
        g_buf[:, columns(slot, rows)] = lax.dot_general(m_buf[...], w_buf[slot], NT, preferred_element_type=jnp.float32).astype(BF)
        for half in range(rows // HD):
            head = slot * (rows // HD) + half

            @pl.when(head != seq)
            def _():
                give(head, seq).start()

            @pl.when(head == seq)
            def _():
                own_g().start()

    own_w.wait()
    ring.run(use, late)
    own_c.wait()

    @pl.loop(1, ndp)
    def _(step):
        sides(step).wait()

    @pl.loop(0, ndp)
    def _(slot):
        store(slot).wait()

    for which in range(3):
        for step in range(nseq - 1):
            spread(which, step).wait()
        keep(which).wait()

    own_g().wait()

    @pl.loop(0, nseq)
    def _(other):
        @pl.when(other != seq)
        def _():
            give(other, seq).wait_send()
            give(other, other).wait_recv()


def bring_in(mask, q, k, v, w, m):
    ndp, nseq = lax.axis_size("dp"), lax.axis_size("seq")
    mine, width = q.shape
    rows = w.shape[0]
    pieces = rows // PIECE
    place = pl.BlockSpec(memory_space=pl.ANY)
    head = jax.ShapeDtypeStruct((mine * nseq, HD), BF)
    dma = pltpu.SemaphoreType.DMA
    return pl.pallas_call(
        bring,
        out_shape=(head,) * 4 + (jax.ShapeDtypeStruct((ndp, rows, width), BF), jax.ShapeDtypeStruct((ndp, mine, rows), BF)),
        in_specs=[pl.BlockSpec(memory_space=pltpu.VMEM)] + [place] * 5,
        out_specs=(place,) * 6,
        scratch_shapes=[
            pltpu.VMEM((ndp, rows, width), BF), pltpu.VMEM((mine, width), BF), pltpu.VMEM((mine, width), BF),
            dma((4, nseq)), dma((4, nseq)), dma((3, pieces)), dma((3, pieces)), dma((4, pieces)), dma((4, pieces)), dma((ndp,)), dma((ndp,)), dma((7,)), dma((ndp,))],
        compiler_params=pltpu.CompilerParams(collective_id=0, has_side_effects=True, vmem_limit_bytes=60 * 2**20),
        name="bring_in",
    )(mask, q, k, v, w, m)


def take(factor, o_ref, dq_ref, dk_ref, dv_ref, wf_ref, mc_ref, out_ref, oq_ref, ok_ref, ov_ref, wg_ref,
         a_buf, w_buf, c_buf, ct_buf, p_buf, part_buf, out_buf, wg_buf,
         o_send, o_recv, g_send, g_recv, r_send, r_recv, f_send, f_recv, p_send, p_recv, local):
    dp, seq = lax.axis_index("dp"), lax.axis_index("seq")
    ndp, nseq = lax.axis_size("dp"), lax.axis_size("seq")
    chips = ndp // 2
    z, core = dp // 2, lax.rem(dp, 2)
    mine, width = a_buf.shape[1:]
    rows = width // ndp
    turns = nseq // 2
    wide = 2 * HD
    tensors = ((dq_ref, oq_ref), (dk_ref, ok_ref), (dv_ref, ov_ref))
    greet(dp, seq, ndp, nseq)

    def slot(offset, other=False):
        return lax.rem(z + chips + offset, chips) * 2 + (1 - core if other else core)

    def pair_at(step):
        return lax.rem(seq // SIDE + SIDE - lax.rem(step, SIDE), SIDE) * 2 + lax.rem(lax.rem(seq, SIDE) // 2 + step // SIDE, 2)

    def target(step):
        turn = step // 2
        return (lax.rem(seq // SIDE + lax.rem(turn, SIDE), SIDE) * 2 + lax.rem(lax.rem(seq, SIDE) // 2 + turn // SIDE, 2)) * 2 + lax.rem(step, 2)

    def home(other, source):
        return pltpu.make_async_remote_copy(o_ref.at[columns(other, mine), :], a_buf.at[dp].at[:, columns(source, HD)],
                                            o_send.at[other], o_recv.at[source], device_id=(dp, other), device_id_type=MESH)

    def hop(kind, step):
        way = (1, -1, 1 - 2 * lax.rem(step, 2))[kind]
        origin = slot(0) if kind < 2 else slot(-way)
        piece = a_buf.at[origin].at[:, columns(pair_at(step), wide)]
        return pltpu.make_async_remote_copy(piece, piece, r_send.at[kind, step], r_recv.at[kind, step],
                                            device_id=(slot(way), seq), device_id_type=MESH)

    def hand(kind, step):
        piece = a_buf.at[slot((0, -1, 1, 2)[kind])].at[:, columns(pair_at(step), wide)]
        return pltpu.make_async_remote_copy(piece, piece, f_send.at[kind, step], f_recv.at[kind, step],
                                            device_id=(slot(0, True), seq), device_id_type=MESH)

    def spread(which, step):
        src, dst = tensors[which]
        other = shifted(seq, step)
        return pltpu.make_async_remote_copy(src.at[columns(other, mine), :], dst.at[:, columns(seq, HD)],
                                            g_send.at[which, step], g_recv.at[which, step], device_id=(dp, other), device_id_type=MESH)

    def keep(which):
        src, dst = tensors[which]
        return pltpu.make_async_copy(src.at[columns(seq, mine), :], dst.at[:, columns(seq, HD)], local.at[which])

    def share(head, source):
        return pltpu.make_async_remote_copy(p_buf.at[:, columns(head, HD)], part_buf.at[source],
                                            p_send.at[head], p_recv.at[source], device_id=(dp, head), device_id_type=MESH)

    own_p = pltpu.make_async_copy(p_buf.at[:, columns(seq, HD)], part_buf.at[seq], local.at[7])
    own_o = pltpu.make_async_copy(o_ref.at[columns(seq, mine), :], a_buf.at[dp].at[:, columns(seq, HD)], local.at[3])
    own_c = pltpu.make_async_copy(mc_ref, c_buf, local.at[4])
    own_w = pltpu.make_async_copy(wf_ref, w_buf, local.at[5])
    own_out = pltpu.make_async_copy(out_buf, out_ref, local.at[6])
    own_o.start()

    @pl.loop(0, nseq)
    def _(step):
        @pl.when(target(step) != seq)
        def _():
            home(target(step), seq).start()

    own_c.start()
    own_w.start()
    for which in range(3):
        for step in range(nseq - 1):
            spread(which, step).start()
        keep(which).start()

    own_c.wait()
    for source in range(ndp):
        ct_buf[:, source * mine:(source + 1) * mine] = c_buf[source].T
    own_o.wait()

    def project(tile):
        at = columns(tile, rows)
        total = jnp.zeros((mine, rows), jnp.float32)
        for source in range(ndp):
            total += jnp.dot(a_buf[dp, :, source * rows:(source + 1) * rows], w_buf[source, :, at], preferred_element_type=jnp.float32)
        out_buf[:, at] = total.astype(BF)

    @pl.loop(0, turns + 3)
    def _(turn):
        @pl.when(turn < turns)
        def _():
            for side in range(2):
                head = pair_at(turn) * 2 + side

                @pl.when(head != seq)
                def _():
                    home(head, head).wait_recv()
            hop(0, turn).start()
            hop(1, turn).start()
            hand(0, turn).start()

        @pl.when((turn >= 1) & (turn < turns + 1))
        def _():
            step = turn - 1
            hop(0, step).wait_recv()
            hop(1, step).wait_recv()
            hop(2, step).start()
            hand(1, step).start()
            hand(2, step).start()

        @pl.when((turn >= 2) & (turn < turns + 2))
        def _():
            step = turn - 2
            hop(2, step).wait_recv()
            hand(3, step).start()

        @pl.when(turn == turns - 1)
        def _():
            own_w.wait()

        @pl.when((turn >= turns - 1) & (turn < turns + 1))
        def _():
            @pl.loop(0, ndp // 2)
            def _(tile):
                project((turn - turns + 1) * (ndp // 2) + tile)

        @pl.when(turn >= 3)
        def _():
            step = turn - 3
            for kind in range(4):
                hand(kind, step).wait_recv()
            at = columns(pair_at(step), wide)
            pieces = a_buf[:, :, at].reshape(ndp * mine, wide)
            p_buf[:, at] = jnp.dot(ct_buf[...], pieces, preferred_element_type=jnp.float32).astype(BF)
            for side in range(2):
                head = pair_at(step) * 2 + side

                @pl.when(head != seq)
                def _():
                    share(head, seq).start()

                @pl.when(head == seq)
                def _():
                    own_p.start()

    own_out.start()
    own_p.wait()
    wg_buf[...] = part_buf[seq].astype(jnp.float32)

    @pl.loop(1, nseq)
    def _(step):
        source = lax.rem(seq + step, nseq)
        share(source, source).wait_recv()
        wg_buf[...] += part_buf[source].astype(jnp.float32)

    wg_ref[...] = wg_buf[...].T * factor
    for which in range(3):
        for step in range(nseq - 1):
            spread(which, step).wait()
        keep(which).wait()

    @pl.loop(1, nseq)
    def _(step):
        home(lax.rem(seq + step, nseq), seq).wait_send()
        share(lax.rem(seq + step, nseq), seq).wait_send()

    @pl.loop(0, turns)
    def _(step):
        for kind in range(3):
            hop(kind, step).wait_send()
        for kind in range(4):
            hand(kind, step).wait_send()
    own_out.wait()


def take_home(o, dq, dk, dv, wf, mc):
    ndp, nseq = lax.axis_size("dp"), lax.axis_size("seq")
    mine, rows = mc.shape[1:]
    width = rows * ndp
    place = pl.BlockSpec(memory_space=pl.ANY)
    out = jax.ShapeDtypeStruct((mine, width), BF)
    dma = pltpu.SemaphoreType.DMA
    factor = 1.0 / math.sqrt(ndp * nseq * mine)
    return pl.pallas_call(
        functools.partial(take, factor),
        out_shape=(out,) * 4 + (jax.ShapeDtypeStruct((HD, rows), jnp.float32),),
        in_specs=[place] * 6,
        out_specs=(place,) * 4 + (pl.BlockSpec(memory_space=pltpu.VMEM),),
        scratch_shapes=[
            pltpu.VMEM((ndp, mine, width), BF), pltpu.VMEM((ndp, rows, width), BF), pltpu.VMEM((ndp, mine, rows), BF),
            pltpu.VMEM((rows, ndp * mine), BF), pltpu.VMEM((rows, width), BF),
            pltpu.VMEM((nseq, rows, HD), BF), pltpu.VMEM((mine, width), BF), pltpu.VMEM((rows, HD), jnp.float32),
            dma((nseq,)), dma((nseq,)), dma((3, nseq)), dma((3, nseq)), dma((3, nseq // 2)), dma((3, nseq // 2)), dma((4, nseq // 2)), dma((4, nseq // 2)),
            dma((nseq,)), dma((nseq,)), dma((8,))],
        compiler_params=pltpu.CompilerParams(collective_id=1, has_side_effects=True, vmem_limit_bytes=60 * 2**20),
        name="take_home",
    )(o, dq, dk, dv, wf, mc)

def attend(pat_ref, live_ref, q_ref, k_ref, v_ref, d_ref, o_ref, dq_ref, dk_ref, dv_ref, kt_ref, vt_ref, acc_ref, e_ref, g_ref, order_ref, fill_ref):
    nb = q_ref.shape[0] // BLOCK
    me = lax.axis_index("seq")
    levels = KMAX // STEP

    def block(index):
        return pl.ds(pl.multiple_of(index * BLOCK, BLOCK), BLOCK)

    def fold(x):
        return x.reshape(-1, 8, x.shape[-1])

    for level in range(levels + 1):
        fill_ref[level] = 0

    @pl.loop(0, nb)
    def _(b):
        fill_ref[(live_ref[me, b] - 1) // STEP + 1] += 1

    for level in range(1, levels):
        fill_ref[level] += fill_ref[level - 1]

    @pl.loop(0, nb)
    def _(b):
        level = (live_ref[me, b] - 1) // STEP
        order_ref[fill_ref[level]] = b
        fill_ref[level] += 1

    @pl.loop(0, nb // UNROLL)
    def _(turn):
        for i in range(UNROLL):
            rows = block(turn * UNROLL + i)
            kt_ref[rows, :] = k_ref[rows, :].T
            vt_ref[rows, :] = v_ref[rows, :].T
            acc_ref[rows, :] = jnp.zeros((BLOCK, 2 * HD), jnp.float32)

    none = jnp.zeros((BLOCK, HD), BF)

    def scores(count, b, at, base):
        live = live_ref[me, b]
        q = q_ref[block(b), :]
        d = d_ref[block(b), :]
        enter = jnp.concatenate([jnp.concatenate([q, none], 1), jnp.concatenate([none, d], 1)], 0)
        top = jnp.full((8, BLOCK), -1e30, jnp.float32)
        total = jnp.zeros((8, BLOCK), jnp.float32)
        mixed = jnp.zeros((8, BLOCK), jnp.float32)
        tops = []
        for j in range(0, count, GROUP):
            many = min(GROUP, count - j)
            both = lax.dot_general(
                jnp.concatenate([jnp.concatenate([k_ref[at[i], :], v_ref[at[i], :]], 1) for i in range(j, j + many)], 0),
                enter, NT, preferred_element_type=jnp.float32)
            s, g = both[:, :BLOCK], both[:, BLOCK:]
            if j + many > 1:
                parts = []
                for i in range(many):
                    part = s[i * BLOCK:(i + 1) * BLOCK]
                    parts.append(jnp.where(j + i < live, part, jnp.float32(-1e30)) if j + i > 0 else part)
                s = jnp.concatenate(parts, 0)
            new = jnp.maximum(top, jnp.max(fold(s), axis=0))
            old = jnp.exp((top - new) * SCALE)
            e = jnp.exp((fold(s) - new[None]) * SCALE)
            total = total * old + jnp.sum(e, axis=0)
            mixed = mixed * old + jnp.sum(e * fold(g), axis=0)
            e_ref[base + j * BLOCK:base + (j + many) * BLOCK, :] = e.reshape(many * BLOCK, BLOCK)
            g_ref[base + j * BLOCK:base + (j + many) * BLOCK, :] = g
            tops += [new] * many
            top = new
        peak = jnp.max(top, axis=0, keepdims=True)
        level = jnp.exp((top - peak) * SCALE)
        inverse = 1.0 / jnp.sum(total * level, axis=0, keepdims=True)
        delta = jnp.sum(mixed * level, axis=0, keepdims=True) * inverse
        return tops, peak, inverse, delta

    def grads(count, b, at, base, tops, peak, inverse, delta):
        q = q_ref[block(b), :]
        d = d_ref[block(b), :]
        leave = jnp.concatenate([jnp.concatenate([d, none], 1), jnp.concatenate([none, q], 1)], 0)
        o_sum = jnp.zeros((HD, BLOCK), jnp.float32)
        q_sum = jnp.zeros((HD, BLOCK), jnp.float32)
        for j in range(0, count, GROUP):
            many = min(GROUP, count - j)
            probs, slopes = [], []
            for i in range(j, j + many):
                e = e_ref[base + i * BLOCK:base + (i + 1) * BLOCK, :]
                g = g_ref[base + i * BLOCK:base + (i + 1) * BLOCK, :]
                weight = jnp.exp((tops[i] - peak) * SCALE) * inverse
                p = (fold(e) * weight[None]).reshape(BLOCK, BLOCK)
                probs.append(p.astype(BF))
                slopes.append((p * (g - delta)).astype(BF))
            pb, sb = jnp.concatenate(probs, 0), jnp.concatenate(slopes, 0)
            ps = jnp.concatenate([pb, sb], 1)
            out = jnp.dot(ps, leave, preferred_element_type=jnp.float32)
            for i in range(many):
                acc_ref[at[j + i], :] += out[i * BLOCK:(i + 1) * BLOCK]
            vt = jnp.concatenate([vt_ref[at[i], :] for i in range(j, j + many)], 1)
            kt = jnp.concatenate([kt_ref[at[i], :] for i in range(j, j + many)], 1)
            two = jnp.dot(jnp.concatenate([vt, kt], 0), ps, preferred_element_type=jnp.float32)
            o_sum += two[:HD, :BLOCK]
            q_sum += two[HD:, BLOCK:]
        o_ref[block(b), :] = o_sum.T.astype(BF)
        dq_ref[block(b), :] = (q_sum.T * SCALE).astype(BF)

    def with_slots(count, turn):
        bs = [order_ref[turn * PAIR + i] for i in range(PAIR)]
        ats = [[block(pat_ref[me, j, b]) for j in range(count)] for b in bs]
        states = [scores(count, b, at, i * KMAX * BLOCK) for i, (b, at) in enumerate(zip(bs, ats))]
        for i, (b, at, state) in enumerate(zip(bs, ats, states)):
            grads(count, b, at, i * KMAX * BLOCK, *state)

    @pl.loop(0, nb // PAIR)
    def _(turn):
        branches = [functools.partial(with_slots, c) for c in range(STEP, KMAX + 1, STEP)]
        longest = live_ref[me, order_ref[turn * PAIR + PAIR - 1]]
        lax.switch((longest - 1) // STEP, branches, turn)

    @pl.loop(0, nb // UNROLL)
    def _(turn):
        for i in range(UNROLL):
            rows = block(turn * UNROLL + i)
            dv_ref[rows, :] = acc_ref[rows, :HD].astype(BF)
            dk_ref[rows, :] = (acc_ref[rows, HD:] * SCALE).astype(BF)


def attention(q, k, v, d, pat, live):
    length = q.shape[0]
    out = jax.ShapeDtypeStruct((length, HD), BF)
    vm = pl.BlockSpec(memory_space=pltpu.VMEM)
    sm = pl.BlockSpec(memory_space=pltpu.SMEM)
    return pl.pallas_call(
        attend,
        out_shape=(out,) * 4,
        in_specs=[sm, sm, vm, vm, vm, vm],
        out_specs=(vm,) * 4,
        scratch_shapes=[
            pltpu.VMEM((length, HD), BF), pltpu.VMEM((length, HD), BF),
            pltpu.VMEM((length, 2 * HD), jnp.float32),
            pltpu.VMEM((PAIR * KMAX * BLOCK, BLOCK), jnp.float32), pltpu.VMEM((PAIR * KMAX * BLOCK, BLOCK), jnp.float32),
            pltpu.SMEM((length // BLOCK,), jnp.int32), pltpu.SMEM((KMAX // STEP + 1,), jnp.int32)],
        compiler_params=pltpu.CompilerParams(vmem_limit_bytes=60 * 2**20),
        name="attention",
    )(pat, live, q, k, v, d)


def pass_on(*refs):
    count = (len(refs) - 1) // 3
    sources, results, stops, sems = refs[:count], refs[count:2 * count], refs[2 * count:3 * count], refs[-1]
    fetches = [pltpu.make_async_copy(sources[i], stops[i], sems.at[0, i]) for i in range(count)]
    stores = [pltpu.make_async_copy(stops[i], results[i], sems.at[1, i]) for i in range(count)]
    for fetch in fetches:
        fetch.start()
    for fetch, store in zip(fetches, stores):
        fetch.wait()
        store.start()
    for store in stores:
        store.wait()


def hand_over(*arrays):
    place = pl.BlockSpec(memory_space=pl.ANY)
    return pl.pallas_call(
        pass_on,
        out_shape=tuple(jax.ShapeDtypeStruct(x.shape, x.dtype) for x in arrays),
        in_specs=[place] * len(arrays),
        out_specs=(place,) * len(arrays),
        scratch_shapes=[pltpu.VMEM(x.shape, x.dtype) for x in arrays] + [pltpu.SemaphoreType.DMA((2, len(arrays)))],
        compiler_params=pltpu.CompilerParams(vmem_limit_bytes=60 * 2**20),
        name="hand_over",
    )(*arrays)


def local(queries, keys, values, weight_out, cotangent, hidden_mask, pattern, live_slots):
    pat = pattern.transpose(0, 2, 1)
    q, k, v, d, weights, sides = bring_in(hidden_mask, queries[0], keys[0], values[0], weight_out, cotangent[0])
    attn, dq, dk, dv = attention(q, k, v, d, pat, live_slots)
    block_out, dq, dk, dv, weight_grad = hand_over(*take_home(attn, dq, dk, dv, weights, sides))
    return (block_out[None], dq[None], dk[None], dv[None], weight_grad)


def solution(mesh):
    rows = P("dp", "seq", None)
    return jax.shard_map(
        local,
        mesh=mesh,
        in_specs=(rows, rows, rows, P("dp", None), rows, P("dp", "seq"), P(), P()),
        out_specs=(rows, rows, rows, rows, P("seq", "dp")),
        check_vma=False,
    )
```

```python
import functools
import math

import jax
import jax.numpy as jnp
from jax import lax
from jax.experimental import pallas as pl
from jax.experimental.pallas import tpu as pltpu
from jax.sharding import PartitionSpec as P

HD = 128
BLOCK = 128
SIDE = 4
PIECE = 32
KMAX = 16
STEP = 2
GROUP = 2
PAIR = 4
UNROLL = 4
SCALE = 1.0 / math.sqrt(HD)
BF = jnp.bfloat16
MESH = pl.DeviceIdType.MESH
NT = (((1,), (1,)), ((), ()))
SHIFTS = ((1, 0), (0, 1), (3, 0), (0, 3), (1, 1), (3, 3), (1, 3), (3, 1), (2, 1), (1, 2), (2, 3), (3, 2), (2, 0), (0, 2), (2, 2))


def shifted(seq, step, back=False):
    dx, dy = SHIFTS[step]
    sign = -1 if back else 1
    return lax.rem(seq // SIDE + SIDE + sign * dx, SIDE) * SIDE + lax.rem(lax.rem(seq, SIDE) + SIDE + sign * dy, SIDE)


def columns(index, width):
    return pl.ds(pl.multiple_of(index * width, width), width)


def greet(dp, seq, ndp, nseq):
    barrier = pltpu.get_barrier_semaphore()

    @pl.loop(1, nseq)
    def _(step):
        pl.semaphore_signal(barrier, inc=1, device_id=(dp, lax.rem(seq + step, nseq)), device_id_type=MESH)

    @pl.loop(1, ndp)
    def _(step):
        pl.semaphore_signal(barrier, inc=1, device_id=(lax.rem(dp + step, ndp), seq), device_id_type=MESH)

    pl.semaphore_wait(barrier, nseq + ndp - 2)


class Ring:
    def __init__(self, shard, buf, dp, seq, ndp, send, recv, give, take):
        self.shard, self.buf, self.dp, self.seq = shard, buf, dp, seq
        self.chips = ndp // 2
        self.pieces = shard.shape[0] // PIECE
        self.z, self.core = dp // 2, lax.rem(dp, 2)
        self.send, self.recv, self.give, self.take = send, recv, give, take

    def slot(self, offset, other=False):
        core = 1 - self.core if other else self.core
        return lax.rem(self.z + self.chips + offset, self.chips) * 2 + core

    def piece(self, ref, index):
        return ref.at[columns(index, PIECE), :]

    def hop(self, kind, index):
        way = (1, -1, 1 - 2 * lax.rem(index, 2))[kind]
        origin = self.slot(0) if kind < 2 else self.slot(-way)
        there = self.piece(self.buf.at[origin], index)
        return pltpu.make_async_remote_copy(self.piece(self.shard, index) if kind < 2 else there, there,
                                            self.send.at[kind, index], self.recv.at[kind, index],
                                            device_id=(self.slot(way), self.seq), device_id_type=MESH)

    def hand(self, kind, index):
        there = self.piece(self.buf.at[self.slot((0, -1, 1, 2)[kind])], index)
        return pltpu.make_async_remote_copy(self.piece(self.shard, index) if kind == 0 else there, there,
                                            self.give.at[kind, index], self.take.at[kind, index],
                                            device_id=(self.slot(0, True), self.seq), device_id_type=MESH)

    def start(self):
        @pl.loop(0, self.pieces)
        def _(index):
            self.hop(0, index).start()
            self.hop(1, index).start()

        @pl.loop(0, self.pieces)
        def _(index):
            self.hand(0, index).start()

    def taken(self, *kinds):
        @pl.loop(0, self.pieces)
        def _(index):
            for kind in kinds:
                self.hand(kind, index).wait_recv()

    def run(self, use, late):
        use(self.slot(0))
        self.taken(0)
        use(self.slot(0, True))

        @pl.loop(0, self.pieces)
        def _(index):
            self.hop(0, index).wait_recv()
            self.hop(1, index).wait_recv()
            self.hop(2, index).start()
            self.hand(1, index).start()
            self.hand(2, index).start()

        use(self.slot(-1))
        use(self.slot(1))
        self.taken(1, 2)
        use(self.slot(-1, True))
        use(self.slot(1, True))

        @pl.loop(0, self.pieces)
        def _(index):
            self.hop(2, index).wait_recv()
            self.hand(3, index).start()

        late()
        use(self.slot(2))
        self.taken(3)
        use(self.slot(2, True))

        @pl.loop(0, self.pieces)
        def _(index):
            for kind in range(3):
                self.hop(kind, index).wait_send()
            for kind in range(4):
                self.hand(kind, index).wait_send()


def bring(mask_ref, q_ref, k_ref, v_ref, w_ref, m_ref, hq_ref, hk_ref, hv_ref, hd_ref, wf_ref, mc_ref,
          w_buf, m_buf, g_buf, a_send, a_recv, w_send, w_recv, f_send, f_recv, m_send, m_recv, local, keep_w):
    dp, seq = lax.axis_index("dp"), lax.axis_index("seq")
    ndp, nseq = lax.axis_size("dp"), lax.axis_size("seq")
    rows, mine = w_ref.shape[0], q_ref.shape[0]
    tensors = ((q_ref, hq_ref), (k_ref, hk_ref), (v_ref, hv_ref))
    greet(dp, seq, ndp, nseq)

    ring = Ring(w_ref, w_buf, dp, seq, ndp, w_send, w_recv, f_send, f_recv)

    def sides(step):
        other = lax.rem(dp + step, ndp)
        return pltpu.make_async_remote_copy(m_buf.at[:, columns(other, rows)], mc_ref.at[dp], m_send.at[step], m_recv.at[step],
                                            device_id=(other, seq), device_id_type=MESH)

    def spread(which, step):
        src, dst = tensors[which]
        other = shifted(seq, step)
        return pltpu.make_async_remote_copy(src.at[:, columns(other, HD)], dst.at[columns(seq, mine), :],
                                            a_send.at[which, step], a_recv.at[which, step], device_id=(dp, other), device_id_type=MESH)

    def keep(which):
        src, dst = tensors[which]
        return pltpu.make_async_copy(src.at[:, columns(seq, HD)], dst.at[columns(seq, mine), :], local.at[which])

    own_w = pltpu.make_async_copy(w_ref, w_buf.at[dp], local.at[3])
    own_m = pltpu.make_async_copy(m_ref, m_buf, local.at[4])
    own_c = pltpu.make_async_copy(m_buf.at[:, columns(dp, rows)], mc_ref.at[dp], local.at[5])
    own_w.start()
    own_m.start()
    ring.start()
    for which in range(3):
        for step in range(nseq - 1):
            spread(which, (step + 5 * which) % (nseq - 1)).start()
        keep(which).start()
    own_m.wait()
    for first in range(0, mine, HD):
        seen = jnp.broadcast_to(mask_ref[:, first:first + HD].astype(jnp.float32), (HD, HD)).T.astype(BF)
        for left in range(0, m_buf.shape[1], HD):
            m_buf[first:first + HD, left:left + HD] *= seen
    own_c.start()

    def late():
        @pl.loop(1, ndp)
        def _(step):
            sides(step).start()

    def store(slot):
        return pltpu.make_async_copy(w_buf.at[slot], wf_ref.at[slot], keep_w.at[slot])

    def give(head, source):
        return pltpu.make_async_remote_copy(g_buf.at[:, columns(head, HD)], hd_ref.at[columns(source, mine), :],
                                            a_send.at[3, head], a_recv.at[3, source], device_id=(dp, head), device_id_type=MESH)

    def own_g():
        return pltpu.make_async_copy(g_buf.at[:, columns(seq, HD)], hd_ref.at[columns(seq, mine), :], local.at[6])

    def use(slot):
        store(slot).start()
        g_buf[:, columns(slot, rows)] = lax.dot_general(m_buf[...], w_buf[slot], NT, preferred_element_type=jnp.float32).astype(BF)
        for half in range(rows // HD):
            head = slot * (rows // HD) + half

            @pl.when(head != seq)
            def _():
                give(head, seq).start()

            @pl.when(head == seq)
            def _():
                own_g().start()

    own_w.wait()
    ring.run(use, late)
    own_c.wait()

    @pl.loop(1, ndp)
    def _(step):
        sides(step).wait()

    @pl.loop(0, ndp)
    def _(slot):
        store(slot).wait()

    for which in range(3):
        for step in range(nseq - 1):
            spread(which, step).wait()
        keep(which).wait()

    own_g().wait()

    @pl.loop(0, nseq)
    def _(other):
        @pl.when(other != seq)
        def _():
            give(other, seq).wait_send()
            give(other, other).wait_recv()


def bring_in(mask, q, k, v, w, m):
    ndp, nseq = lax.axis_size("dp"), lax.axis_size("seq")
    mine, width = q.shape
    rows = w.shape[0]
    pieces = rows // PIECE
    place = pl.BlockSpec(memory_space=pl.ANY)
    head = jax.ShapeDtypeStruct((mine * nseq, HD), BF)
    dma = pltpu.SemaphoreType.DMA
    return pl.pallas_call(
        bring,
        out_shape=(head,) * 4 + (jax.ShapeDtypeStruct((ndp, rows, width), BF), jax.ShapeDtypeStruct((ndp, mine, rows), BF)),
        in_specs=[pl.BlockSpec(memory_space=pltpu.VMEM)] + [place] * 5,
        out_specs=(place,) * 6,
        scratch_shapes=[
            pltpu.VMEM((ndp, rows, width), BF), pltpu.VMEM((mine, width), BF), pltpu.VMEM((mine, width), BF),
            dma((4, nseq)), dma((4, nseq)), dma((3, pieces)), dma((3, pieces)), dma((4, pieces)), dma((4, pieces)), dma((ndp,)), dma((ndp,)), dma((7,)), dma((ndp,))],
        compiler_params=pltpu.CompilerParams(collective_id=0, has_side_effects=True, vmem_limit_bytes=60 * 2**20),
        name="bring_in",
    )(mask, q, k, v, w, m)


def take(factor, o_ref, dq_ref, dk_ref, dv_ref, wf_ref, mc_ref, out_ref, oq_ref, ok_ref, ov_ref, wg_ref,
         a_buf, w_buf, c_buf, ct_buf, p_buf, part_buf, out_buf, wg_buf,
         o_send, o_recv, g_send, g_recv, r_send, r_recv, f_send, f_recv, p_send, p_recv, local):
    dp, seq = lax.axis_index("dp"), lax.axis_index("seq")
    ndp, nseq = lax.axis_size("dp"), lax.axis_size("seq")
    chips = ndp // 2
    z, core = dp // 2, lax.rem(dp, 2)
    mine, width = a_buf.shape[1:]
    rows = width // ndp
    turns = nseq // 2
    wide = 2 * HD
    tensors = ((dq_ref, oq_ref), (dk_ref, ok_ref), (dv_ref, ov_ref))
    greet(dp, seq, ndp, nseq)

    def slot(offset, other=False):
        return lax.rem(z + chips + offset, chips) * 2 + (1 - core if other else core)

    def pair_at(step):
        return lax.rem(seq // SIDE + SIDE - lax.rem(step, SIDE), SIDE) * 2 + lax.rem(lax.rem(seq, SIDE) // 2 + step // SIDE, 2)

    def target(step):
        turn = step // 2
        return (lax.rem(seq // SIDE + lax.rem(turn, SIDE), SIDE) * 2 + lax.rem(lax.rem(seq, SIDE) // 2 + turn // SIDE, 2)) * 2 + lax.rem(step, 2)

    def home(other, source):
        return pltpu.make_async_remote_copy(o_ref.at[columns(other, mine), :], a_buf.at[dp].at[:, columns(source, HD)],
                                            o_send.at[other], o_recv.at[source], device_id=(dp, other), device_id_type=MESH)

    def hop(kind, step):
        way = (1, -1, 1 - 2 * lax.rem(step, 2))[kind]
        origin = slot(0) if kind < 2 else slot(-way)
        piece = a_buf.at[origin].at[:, columns(pair_at(step), wide)]
        return pltpu.make_async_remote_copy(piece, piece, r_send.at[kind, step], r_recv.at[kind, step],
                                            device_id=(slot(way), seq), device_id_type=MESH)

    def hand(kind, step):
        piece = a_buf.at[slot((0, -1, 1, 2)[kind])].at[:, columns(pair_at(step), wide)]
        return pltpu.make_async_remote_copy(piece, piece, f_send.at[kind, step], f_recv.at[kind, step],
                                            device_id=(slot(0, True), seq), device_id_type=MESH)

    def spread(which, step):
        src, dst = tensors[which]
        other = shifted(seq, step)
        return pltpu.make_async_remote_copy(src.at[columns(other, mine), :], dst.at[:, columns(seq, HD)],
                                            g_send.at[which, step], g_recv.at[which, step], device_id=(dp, other), device_id_type=MESH)

    def keep(which):
        src, dst = tensors[which]
        return pltpu.make_async_copy(src.at[columns(seq, mine), :], dst.at[:, columns(seq, HD)], local.at[which])

    def share(head, source):
        return pltpu.make_async_remote_copy(p_buf.at[:, columns(head, HD)], part_buf.at[source],
                                            p_send.at[head], p_recv.at[source], device_id=(dp, head), device_id_type=MESH)

    own_p = pltpu.make_async_copy(p_buf.at[:, columns(seq, HD)], part_buf.at[seq], local.at[7])
    own_o = pltpu.make_async_copy(o_ref.at[columns(seq, mine), :], a_buf.at[dp].at[:, columns(seq, HD)], local.at[3])
    own_c = pltpu.make_async_copy(mc_ref, c_buf, local.at[4])
    own_w = pltpu.make_async_copy(wf_ref, w_buf, local.at[5])
    own_out = pltpu.make_async_copy(out_buf, out_ref, local.at[6])
    own_o.start()

    @pl.loop(0, nseq)
    def _(step):
        @pl.when(target(step) != seq)
        def _():
            home(target(step), seq).start()

    own_c.start()
    own_w.start()
    for which in range(3):
        for step in range(nseq - 1):
            spread(which, (step + 5 * which) % (nseq - 1)).start()
        keep(which).start()

    own_c.wait()
    for source in range(ndp):
        ct_buf[:, source * mine:(source + 1) * mine] = c_buf[source].T
    own_o.wait()

    def project(tile):
        at = columns(tile, rows)
        total = jnp.zeros((mine, rows), jnp.float32)
        for source in range(ndp):
            total += jnp.dot(a_buf[dp, :, source * rows:(source + 1) * rows], w_buf[source, :, at], preferred_element_type=jnp.float32)
        out_buf[:, at] = total.astype(BF)

    @pl.loop(0, turns + 3)
    def _(turn):
        @pl.when(turn < turns)
        def _():
            for side in range(2):
                head = pair_at(turn) * 2 + side

                @pl.when(head != seq)
                def _():
                    home(head, head).wait_recv()
            hop(0, turn).start()
            hop(1, turn).start()
            hand(0, turn).start()

        @pl.when((turn >= 1) & (turn < turns + 1))
        def _():
            step = turn - 1
            hop(0, step).wait_recv()
            hop(1, step).wait_recv()
            hop(2, step).start()
            hand(1, step).start()
            hand(2, step).start()

        @pl.when((turn >= 2) & (turn < turns + 2))
        def _():
            step = turn - 2
            hop(2, step).wait_recv()
            hand(3, step).start()

        @pl.when(turn == turns - 1)
        def _():
            own_w.wait()

        @pl.when((turn >= turns - 1) & (turn < turns + 1))
        def _():
            @pl.loop(0, ndp // 2)
            def _(tile):
                project((turn - turns + 1) * (ndp // 2) + tile)

        @pl.when(turn >= 3)
        def _():
            step = turn - 3
            for kind in range(4):
                hand(kind, step).wait_recv()
            at = columns(pair_at(step), wide)
            pieces = a_buf[:, :, at].reshape(ndp * mine, wide)
            p_buf[:, at] = jnp.dot(ct_buf[...], pieces, preferred_element_type=jnp.float32).astype(BF)
            for side in range(2):
                head = pair_at(step) * 2 + side

                @pl.when(head != seq)
                def _():
                    share(head, seq).start()

                @pl.when(head == seq)
                def _():
                    own_p.start()

    own_out.start()
    own_p.wait()
    wg_buf[...] = part_buf[seq].astype(jnp.float32)

    @pl.loop(1, nseq)
    def _(step):
        source = lax.rem(seq + step, nseq)
        share(source, source).wait_recv()
        wg_buf[...] += part_buf[source].astype(jnp.float32)

    wg_ref[...] = wg_buf[...].T * factor
    for which in range(3):
        for step in range(nseq - 1):
            spread(which, step).wait()
        keep(which).wait()

    @pl.loop(1, nseq)
    def _(step):
        home(lax.rem(seq + step, nseq), seq).wait_send()
        share(lax.rem(seq + step, nseq), seq).wait_send()

    @pl.loop(0, turns)
    def _(step):
        for kind in range(3):
            hop(kind, step).wait_send()
        for kind in range(4):
            hand(kind, step).wait_send()
    own_out.wait()


def take_home(o, dq, dk, dv, wf, mc):
    ndp, nseq = lax.axis_size("dp"), lax.axis_size("seq")
    mine, rows = mc.shape[1:]
    width = rows * ndp
    place = pl.BlockSpec(memory_space=pl.ANY)
    out = jax.ShapeDtypeStruct((mine, width), BF)
    dma = pltpu.SemaphoreType.DMA
    factor = 1.0 / math.sqrt(ndp * nseq * mine)
    return pl.pallas_call(
        functools.partial(take, factor),
        out_shape=(out,) * 4 + (jax.ShapeDtypeStruct((HD, rows), jnp.float32),),
        in_specs=[place] * 6,
        out_specs=(place,) * 4 + (pl.BlockSpec(memory_space=pltpu.VMEM),),
        scratch_shapes=[
            pltpu.VMEM((ndp, mine, width), BF), pltpu.VMEM((ndp, rows, width), BF), pltpu.VMEM((ndp, mine, rows), BF),
            pltpu.VMEM((rows, ndp * mine), BF), pltpu.VMEM((rows, width), BF),
            pltpu.VMEM((nseq, rows, HD), BF), pltpu.VMEM((mine, width), BF), pltpu.VMEM((rows, HD), jnp.float32),
            dma((nseq,)), dma((nseq,)), dma((3, nseq)), dma((3, nseq)), dma((3, nseq // 2)), dma((3, nseq // 2)), dma((4, nseq // 2)), dma((4, nseq // 2)),
            dma((nseq,)), dma((nseq,)), dma((8,))],
        compiler_params=pltpu.CompilerParams(collective_id=1, has_side_effects=True, vmem_limit_bytes=60 * 2**20),
        name="take_home",
    )(o, dq, dk, dv, wf, mc)

def attend(pat_ref, live_ref, q_ref, k_ref, v_ref, d_ref, o_ref, dq_ref, dk_ref, dv_ref, kt_ref, vt_ref, acc_ref, e_ref, g_ref, order_ref, fill_ref):
    nb = q_ref.shape[0] // BLOCK
    me = lax.axis_index("seq")
    levels = KMAX // STEP

    def block(index):
        return pl.ds(pl.multiple_of(index * BLOCK, BLOCK), BLOCK)

    def fold(x):
        return x.reshape(-1, 8, x.shape[-1])

    for level in range(levels + 1):
        fill_ref[level] = 0

    @pl.loop(0, nb)
    def _(b):
        fill_ref[(live_ref[me, b] - 1) // STEP + 1] += 1

    for level in range(1, levels):
        fill_ref[level] += fill_ref[level - 1]

    @pl.loop(0, nb)
    def _(b):
        level = (live_ref[me, b] - 1) // STEP
        order_ref[fill_ref[level]] = b
        fill_ref[level] += 1

    @pl.loop(0, nb // UNROLL)
    def _(turn):
        for i in range(UNROLL):
            rows = block(turn * UNROLL + i)
            kt_ref[rows, :] = k_ref[rows, :].T
            vt_ref[rows, :] = v_ref[rows, :].T
            acc_ref[rows, :] = jnp.zeros((BLOCK, 2 * HD), jnp.float32)

    none = jnp.zeros((BLOCK, HD), BF)

    def scores(count, b, at, base):
        live = live_ref[me, b]
        q = q_ref[block(b), :]
        d = d_ref[block(b), :]
        enter = jnp.concatenate([jnp.concatenate([q, none], 1), jnp.concatenate([none, d], 1)], 0)
        top = jnp.full((8, BLOCK), -1e30, jnp.float32)
        total = jnp.zeros((8, BLOCK), jnp.float32)
        mixed = jnp.zeros((8, BLOCK), jnp.float32)
        tops = []
        for j in range(0, count, GROUP):
            many = min(GROUP, count - j)
            both = lax.dot_general(
                jnp.concatenate([jnp.concatenate([k_ref[at[i], :], v_ref[at[i], :]], 1) for i in range(j, j + many)], 0),
                enter, NT, preferred_element_type=jnp.float32)
            s, g = both[:, :BLOCK], both[:, BLOCK:]
            if j + many > 1:
                parts = []
                for i in range(many):
                    part = s[i * BLOCK:(i + 1) * BLOCK]
                    parts.append(jnp.where(j + i < live, part, jnp.float32(-1e30)) if j + i > 0 else part)
                s = jnp.concatenate(parts, 0)
            new = jnp.maximum(top, jnp.max(fold(s), axis=0))
            old = jnp.exp((top - new) * SCALE)
            e = jnp.exp((fold(s) - new[None]) * SCALE)
            total = total * old + jnp.sum(e, axis=0)
            mixed = mixed * old + jnp.sum(e * fold(g), axis=0)
            e_ref[base + j * BLOCK:base + (j + many) * BLOCK, :] = e.reshape(many * BLOCK, BLOCK)
            g_ref[base + j * BLOCK:base + (j + many) * BLOCK, :] = g
            tops += [new] * many
            top = new
        peak = jnp.max(top, axis=0, keepdims=True)
        level = jnp.exp((top - peak) * SCALE)
        inverse = 1.0 / jnp.sum(total * level, axis=0, keepdims=True)
        delta = jnp.sum(mixed * level, axis=0, keepdims=True) * inverse
        return tops, peak, inverse, delta

    def grads(count, b, at, base, tops, peak, inverse, delta):
        q = q_ref[block(b), :]
        d = d_ref[block(b), :]
        leave = jnp.concatenate([jnp.concatenate([d, none], 1), jnp.concatenate([none, q], 1)], 0)
        o_sum = jnp.zeros((HD, BLOCK), jnp.float32)
        q_sum = jnp.zeros((HD, BLOCK), jnp.float32)
        for j in range(0, count, GROUP):
            many = min(GROUP, count - j)
            probs, slopes = [], []
            for i in range(j, j + many):
                e = e_ref[base + i * BLOCK:base + (i + 1) * BLOCK, :]
                g = g_ref[base + i * BLOCK:base + (i + 1) * BLOCK, :]
                weight = jnp.exp((tops[i] - peak) * SCALE) * inverse
                p = (fold(e) * weight[None]).reshape(BLOCK, BLOCK)
                probs.append(p.astype(BF))
                slopes.append((p * (g - delta)).astype(BF))
            pb, sb = jnp.concatenate(probs, 0), jnp.concatenate(slopes, 0)
            ps = jnp.concatenate([pb, sb], 1)
            out = jnp.dot(ps, leave, preferred_element_type=jnp.float32)
            for i in range(many):
                acc_ref[at[j + i], :] += out[i * BLOCK:(i + 1) * BLOCK]
            vt = jnp.concatenate([vt_ref[at[i], :] for i in range(j, j + many)], 1)
            kt = jnp.concatenate([kt_ref[at[i], :] for i in range(j, j + many)], 1)
            two = jnp.dot(jnp.concatenate([vt, kt], 0), ps, preferred_element_type=jnp.float32)
            o_sum += two[:HD, :BLOCK]
            q_sum += two[HD:, BLOCK:]
        o_ref[block(b), :] = o_sum.T.astype(BF)
        dq_ref[block(b), :] = (q_sum.T * SCALE).astype(BF)

    def with_slots(count, turn):
        bs = [order_ref[turn * PAIR + i] for i in range(PAIR)]
        ats = [[block(pat_ref[me, j, b]) for j in range(count)] for b in bs]
        states = [scores(count, b, at, i * KMAX * BLOCK) for i, (b, at) in enumerate(zip(bs, ats))]
        for i, (b, at, state) in enumerate(zip(bs, ats, states)):
            grads(count, b, at, i * KMAX * BLOCK, *state)

    @pl.loop(0, nb // PAIR)
    def _(turn):
        branches = [functools.partial(with_slots, c) for c in range(STEP, KMAX + 1, STEP)]
        longest = live_ref[me, order_ref[turn * PAIR + PAIR - 1]]
        lax.switch((longest - 1) // STEP, branches, turn)

    @pl.loop(0, nb // UNROLL)
    def _(turn):
        for i in range(UNROLL):
            rows = block(turn * UNROLL + i)
            dv_ref[rows, :] = acc_ref[rows, :HD].astype(BF)
            dk_ref[rows, :] = (acc_ref[rows, HD:] * SCALE).astype(BF)


def attention(q, k, v, d, pat, live):
    length = q.shape[0]
    out = jax.ShapeDtypeStruct((length, HD), BF)
    vm = pl.BlockSpec(memory_space=pltpu.VMEM)
    sm = pl.BlockSpec(memory_space=pltpu.SMEM)
    return pl.pallas_call(
        attend,
        out_shape=(out,) * 4,
        in_specs=[sm, sm, vm, vm, vm, vm],
        out_specs=(vm,) * 4,
        scratch_shapes=[
            pltpu.VMEM((length, HD), BF), pltpu.VMEM((length, HD), BF),
            pltpu.VMEM((length, 2 * HD), jnp.float32),
            pltpu.VMEM((PAIR * KMAX * BLOCK, BLOCK), jnp.float32), pltpu.VMEM((PAIR * KMAX * BLOCK, BLOCK), jnp.float32),
            pltpu.SMEM((length // BLOCK,), jnp.int32), pltpu.SMEM((KMAX // STEP + 1,), jnp.int32)],
        compiler_params=pltpu.CompilerParams(vmem_limit_bytes=60 * 2**20),
        name="attention",
    )(pat, live, q, k, v, d)


def pass_on(*refs):
    count = (len(refs) - 1) // 3
    sources, results, stops, sems = refs[:count], refs[count:2 * count], refs[2 * count:3 * count], refs[-1]
    fetches = [pltpu.make_async_copy(sources[i], stops[i], sems.at[0, i]) for i in range(count)]
    stores = [pltpu.make_async_copy(stops[i], results[i], sems.at[1, i]) for i in range(count)]
    for fetch in fetches:
        fetch.start()
    for fetch, store in zip(fetches, stores):
        fetch.wait()
        store.start()
    for store in stores:
        store.wait()


def hand_over(*arrays):
    place = pl.BlockSpec(memory_space=pl.ANY)
    return pl.pallas_call(
        pass_on,
        out_shape=tuple(jax.ShapeDtypeStruct(x.shape, x.dtype) for x in arrays),
        in_specs=[place] * len(arrays),
        out_specs=(place,) * len(arrays),
        scratch_shapes=[pltpu.VMEM(x.shape, x.dtype) for x in arrays] + [pltpu.SemaphoreType.DMA((2, len(arrays)))],
        compiler_params=pltpu.CompilerParams(vmem_limit_bytes=60 * 2**20),
        name="hand_over",
    )(*arrays)


def local(queries, keys, values, weight_out, cotangent, hidden_mask, pattern, live_slots):
    pat = pattern.transpose(0, 2, 1)
    q, k, v, d, weights, sides = bring_in(hidden_mask, queries[0], keys[0], values[0], weight_out, cotangent[0])
    attn, dq, dk, dv = attention(q, k, v, d, pat, live_slots)
    block_out, dq, dk, dv, weight_grad = hand_over(*take_home(attn, dq, dk, dv, weights, sides))
    return (block_out[None], dq[None], dk[None], dv[None], weight_grad)


def solution(mesh):
    rows = P("dp", "seq", None)
    return jax.shard_map(
        local,
        mesh=mesh,
        in_specs=(rows, rows, rows, P("dp", None), rows, P("dp", "seq"), P(), P()),
        out_specs=(rows, rows, rows, rows, P("seq", "dp")),
        check_vma=False,
    )
```
